32 devices in a mesh: slide: 8 (over z, x), band: 4 (over y, core).
Axes of the slice: x: 2, y: 2, z: 4, core: 2. Of those that a mesh axis runs over, the one named last changes fastest.
Arguments:
- queries: bfloat16 [16384, 1536], P(('slide', 'band')), parts along dimension 0, may hold values from -200 to 200
- keys: bfloat16 [16384, 1536], P(('slide', 'band')), parts along dimension 0, may hold values from -8 to 8
- values: bfloat16 [16384, 1536], P(('slide', 'band')), parts along dimension 0, may hold values from -6 to 6
- out_gain: float32 [1536], replicated, may hold values from 0.1 to 1.9
- out_weight: bfloat16 [1536, 1536], replicated, may hold values from -0.15625 to 0.15625
- adjacency: int32 [32, 2, 256], P(('slide', 'band')), parts along dimension 0, may hold values from 0 to 511, as said below
- send_counts: int32 [32, 2], P('slide'), parts along dimension 0, may hold values from 1 to 256
- coarse_index: int32 [1024], P(('slide', 'band')), parts along dimension 0, may hold values from 0 to 511, as said below
Outputs:
- context: bfloat16 [16384, 1536], P(('slide', 'band')), parts along dimension 0
The draws below stay inside these ranges and needn't reach their ends.
There are 8 independent parts, one for each index of `slide`. The reference program is written for one: setup_inputs(seed, part) draws one part's arguments, and reference() takes and returns one part's arrays. A program takes and returns all parts, laid end to end along the dimension named above; an argument that names none is the same for every part. Nothing has to cross between parts.
Inputs may be any that keep to these rules, and one draw needn't show every extreme that they name: Within a band, adjacency side 0 lists rows from the first half of the band, side 1 from the second half; entries may repeat; entries at positions from the live count on are padding. `coarse_index`: entry r of a band's block lies in r * 16 to r * 16 + 15.
All inputs are finite; a program needn't handle non-finite values.
Results may differ from the reference program's by a relative error of at most 0.0085.
Values may be sent and summed in bfloat16 or wider, within the bound.
No kernel may reach another device: no remote copies, remote signals or barrier semaphores. Data moves between devices by JAX's collectives and lax.ppermute only.
A program may use at most 128 MiB of HBM per device.

```python
import math
import jax
import jax.numpy as jnp
from jax import lax

H = 12
HD = 128
D = 1536
TOK_DEV = 512
DILATION = 16
BMAX = 256
CK = 32
NBANDS = 4
NT = 2048
NC = 128


def shared_pair(key):
    key_draw = jax.random.fold_in(key, 11)
    query_draw = jax.random.fold_in(key, 12)
    key_rows = jnp.clip(jax.random.normal(key_draw, (NT, D), jnp.float32), -6.0, 6.0)
    query_rows = jnp.clip(jax.random.normal(query_draw, (NT, D), jnp.float32), -6.0, 6.0)
    return (query_rows, key_rows)


def draw_queries(key, part):
    return shared_pair(key)[0].astype(jnp.bfloat16)


def draw_keys(key, part):
    return shared_pair(key)[1].astype(jnp.bfloat16)


def boundary_tables(key):
    count_draw = jax.random.fold_in(key, 21)
    pick_draw = jax.random.fold_in(key, 22)
    lower_draw = jax.random.fold_in(key, 23)
    upper_draw = jax.random.fold_in(key, 24)
    counts = jax.random.randint(count_draw, (NBANDS * 2,), 1, BMAX + 1)
    spot = jax.random.randint(pick_draw, (), 0, NBANDS * 2)
    counts = counts.at[spot].set(BMAX).at[(spot + 1) % (NBANDS * 2)].set(1)
    lower = jax.random.randint(lower_draw, (NBANDS, BMAX), 0, TOK_DEV // 2).at[:, 0].set(0)
    upper = jax.random.randint(upper_draw, (NBANDS, BMAX), TOK_DEV // 2, TOK_DEV).at[:, 0].set(TOK_DEV - 1)
    return (jnp.stack([lower, upper], axis=1).astype(jnp.int32), counts.reshape(NBANDS, 2).astype(jnp.int32))


def draw_adjacency(key, part):
    return boundary_tables(key)[0]


def draw_send_counts(key, part):
    return boundary_tables(key)[1]


def draw_coarse_index(key, part):
    offsets = jax.random.randint(jax.random.fold_in(key, 31), (NBANDS, CK), 0, DILATION)
    first_band = jax.random.randint(jax.random.fold_in(key, 32), (), 0, NBANDS)
    last_band = (first_band + 1 + jax.random.randint(jax.random.fold_in(key, 33), (), 0, NBANDS - 1)) % NBANDS
    offsets = offsets.at[first_band, 0].set(0).at[last_band, CK - 1].set(DILATION - 1)
    picked = DILATION * jnp.arange(CK, dtype=jnp.int32)[None, :] + offsets
    return picked.reshape(NC).astype(jnp.int32)


def block_levels(stream_key, dims, shards, least, largest):
    factor_of, own = 1.0, jax.random.fold_in(stream_key, 6)
    for dim, shards_of in shards:
        draws = jnp.exp(jax.random.uniform(jax.random.fold_in(own, dim), (shards_of,), jnp.float32, least / len(shards), largest / len(shards)))
        factor_of = factor_of * jnp.repeat(draws, dims[dim] // shards_of).reshape([-1 if axis == dim else 1 for axis in range(len(dims))])
    return factor_of


def gaussian(stream_key, shape, deviation, bound, shards=(), kind=jnp.bfloat16):
    gain = block_levels(stream_key, shape, shards, -0.22, 0.18) if shards else 1.0
    entries = jax.random.normal(stream_key, shape, jnp.float32) * deviation * gain
    return jnp.minimum(jnp.maximum(entries, -bound), bound).astype(kind)


def setup_inputs(seed: int = 0, part: int = 0) -> dict:
    key_of = jax.random.split(jax.random.key(seed), 9)
    part_splits = jax.random.split(jax.random.fold_in(key_of[8], part), 9)
    return {
        "queries": draw_queries(jax.random.fold_in(jax.random.fold_in(key_of[8], part), 71), part),
        "keys": draw_keys(jax.random.fold_in(jax.random.fold_in(key_of[8], part), 71), part),
        "values": gaussian(part_splits[2], (NT, D), 1.0, 6.0, ((0, 4),)),
        "out_gain": jnp.clip(1.0 + 0.18 * jax.random.normal(key_of[3], (D,), jnp.float32), 0.1, 1.9),
        "out_weight": gaussian(key_of[4], (D, D), D ** -0.5, 0.15625),
        "adjacency": draw_adjacency(jax.random.fold_in(jax.random.fold_in(key_of[8], part), 71), part),
        "send_counts": draw_send_counts(jax.random.fold_in(jax.random.fold_in(key_of[8], part), 71), part),
        "coarse_index": draw_coarse_index(jax.random.fold_in(jax.random.fold_in(key_of[8], part), 71), part),
    }


def reference(queries, keys, values, out_gain, out_weight, adjacency, send_counts, coarse_index):
    coarse_rows = jnp.arange(NC, dtype=jnp.int32) // CK * TOK_DEV + coarse_index.astype(jnp.int32)
    coarse_keys = keys[coarse_rows]
    coarse_values = values[coarse_rows]
    slots = jnp.arange(BMAX, dtype=jnp.int32)
    scale = 1.0 / math.sqrt(HD)

    def one_band(band):
        start = (band * TOK_DEV).astype(jnp.int32)
        query_rows = lax.dynamic_slice_in_dim(queries, start, TOK_DEV, 0)
        local_keys = lax.dynamic_slice_in_dim(keys, start, TOK_DEV, 0)
        local_values = lax.dynamic_slice_in_dim(values, start, TOK_DEV, 0)
        lower = jnp.maximum(band - 1, 0).astype(jnp.int32)
        upper = jnp.minimum(band + 1, NBANDS - 1).astype(jnp.int32)
        lower_rows = lower * TOK_DEV + adjacency[lower, 1]
        upper_rows = upper * TOK_DEV + adjacency[upper, 0]
        lower_live = (slots < send_counts[lower, 1]) & (band > 0)
        upper_live = (slots < send_counts[upper, 0]) & (band < NBANDS - 1)
        all_keys = jnp.concatenate([local_keys, keys[lower_rows], keys[upper_rows], coarse_keys], axis=0)
        all_values = jnp.concatenate([local_values, values[lower_rows], values[upper_rows], coarse_values], axis=0)
        live = jnp.concatenate([jnp.ones((TOK_DEV,), jnp.bool_), lower_live, upper_live, jnp.ones((NC,), jnp.bool_)])
        count = all_keys.shape[0]
        query_heads = query_rows.astype(jnp.float32).reshape(TOK_DEV, H, HD)
        key_heads = all_keys.astype(jnp.float32).reshape(count, H, HD)
        value_heads = all_values.astype(jnp.float32).reshape(count, H, HD)
        scores = jnp.einsum('qhd,khd->hqk', query_heads, key_heads) * scale
        scores = jnp.where(live[None, None, :], scores, -1e+30)
        highest = lax.optimization_barrier(jnp.max(scores, axis=2))
        weights = jnp.exp(scores - highest[:, :, None])
        totals = lax.optimization_barrier(jnp.sum(weights, axis=2))
        rounded = weights.astype(jnp.bfloat16).astype(jnp.float32)
        summed = jnp.einsum('hqk,khd->qhd', rounded, value_heads)
        attended = (summed / jnp.transpose(totals)[:, :, None]).reshape(TOK_DEV, D)
        center = lax.optimization_barrier(jnp.mean(attended, axis=1, keepdims=True))
        shifted = attended - center
        spread = lax.optimization_barrier(jnp.mean(shifted * shifted, axis=1, keepdims=True))
        normed = (shifted / jnp.sqrt(spread + 1e-05) * out_gain.astype(jnp.float32)).astype(jnp.bfloat16)
        return jnp.dot(normed, out_weight, preferred_element_type=jnp.float32).astype(jnp.bfloat16)
    result = lax.map(one_band, jnp.arange(NBANDS, dtype=jnp.int32))
    return result.reshape(NT, D)
```

```python
import functools
import math

import jax
import jax.numpy as jnp
from jax import lax
from jax.experimental import pallas as pl
from jax.experimental.pallas import tpu as pltpu
from jax.sharding import PartitionSpec as P

H = 12
HD = 128
SCALE = math.log2(math.e) / math.sqrt(HD)
DEAD = -1e30
META_LANES = 384

VMEM = pltpu.VMEM
NT = (((1,), (1,)), ((), ()))


def dot(a, b):
    return jnp.dot(a, b, preferred_element_type=jnp.float32)


def dot_nt(a, b):
    return lax.dot_general(a, b, NT, preferred_element_type=jnp.float32)


def column(row):
    n = row.shape[1]
    shape = (n, n)
    diagonal = lax.broadcasted_iota(jnp.int32, shape, 0) == lax.broadcasted_iota(jnp.int32, shape, 1)
    return jnp.sum(jnp.where(diagonal, jnp.broadcast_to(row, shape), 0.0), axis=1, keepdims=True)


def log_mult(mult):
    return jnp.where(mult > 0.0, jnp.log2(jnp.maximum(mult, 1.0)), DEAD)


def coarse_kernel(index_ref, keys_ref, values_ref, out_ref):
    count = index_ref.shape[1]
    rows = keys_ref.shape[0]
    picked = column(index_ref[...].astype(jnp.float32))
    slots = lax.broadcasted_iota(jnp.int32, (count, rows), 1).astype(jnp.float32)
    choose = (picked == slots).astype(jnp.bfloat16)
    out_ref[0:count, :] = dot(choose, keys_ref[...]).astype(jnp.bfloat16)
    out_ref[count : 2 * count, :] = dot(choose, values_ref[...]).astype(jnp.bfloat16)


def multiplicity(adjacency_ref, counts_ref, side, base):
    width = adjacency_ref.shape[2]
    place = lax.axis_index("band")
    live = counts_ref[place, side]
    entries = adjacency_ref[0, pl.ds(side, 1), :].astype(jnp.float32) - base.astype(jnp.float32)
    shape = (width, width)
    slot = lax.broadcasted_iota(jnp.int32, shape, 0)
    row = lax.broadcasted_iota(jnp.int32, shape, 1).astype(jnp.float32)
    hits = jnp.where((column(entries) == row) & (slot < live), 1.0, 0.0)
    return jnp.sum(hits, axis=0, keepdims=True)


def boundary_kernel(adjacency_ref, counts_ref, keys_ref, values_ref, far_keys_ref, far_values_ref, near_mult_ref):
    width = adjacency_ref.shape[2]
    slots = far_keys_ref.shape[0]
    odd = lax.rem(lax.axis_index("band"), 2)
    base = pl.multiple_of(odd * width, width)
    near_mult = multiplicity(adjacency_ref, counts_ref, 1 - odd, (1 - odd) * width)
    near_mult_ref[...] = jnp.broadcast_to(near_mult, near_mult_ref.shape)
    mult = multiplicity(adjacency_ref, counts_ref, odd, base)
    present = (mult > 0.0).astype(jnp.bfloat16)
    square = (width, width)
    before = lax.broadcasted_iota(jnp.int32, square, 0) < lax.broadcasted_iota(jnp.int32, square, 1)
    order = dot(jnp.broadcast_to(present, (16, width)), before.astype(jnp.bfloat16))[0:1, :]
    place = jnp.where(mult > 0.0, order, -1.0)
    wanted = lax.broadcasted_iota(jnp.int32, (slots, width), 0)
    choose = (wanted.astype(jnp.float32) == place) & (wanted < slots - 1)
    choose = jnp.where(choose, 1.0, 0.0).astype(jnp.bfloat16)
    rows = pl.ds(base, width)
    slot_mult = dot_nt(jnp.broadcast_to(mult.astype(jnp.bfloat16), (16, width)), choose)[0:1, :]
    far_keys_ref[...] = dot(choose, keys_ref[rows, :]).astype(jnp.bfloat16)
    meta = jnp.concatenate([slot_mult, jnp.zeros((1, META_LANES - slots), jnp.float32)], axis=1)
    tail = slots - 16
    last = lax.broadcasted_iota(jnp.int32, (16, META_LANES), 0) == 15
    old = far_keys_ref[tail:slots, 0:META_LANES].astype(jnp.float32)
    far_keys_ref[tail:slots, 0:META_LANES] = jnp.where(last, meta, old).astype(jnp.bfloat16)
    far_values_ref[...] = dot(choose, values_ref[rows, :]).astype(jnp.bfloat16)


def head(h):
    return pl.ds(pl.multiple_of(h * HD, HD), HD)


def with_ones(rows):
    return jnp.concatenate([rows, jnp.ones_like(rows)], axis=1)


def put_column(ref, h, col):
    lane = lax.broadcasted_iota(jnp.int32, ref.shape, 1)
    ref[...] = jnp.where(lane == h, col, ref[...])


def get_column(ref, h):
    lane = lax.broadcasted_iota(jnp.int32, ref.shape, 1)
    return jnp.sum(jnp.where(lane == h, ref[...], 0.0), axis=1, keepdims=True)


def own_kernel(queries_ref, keys_ref, values_ref, high_ref, total_ref, accum_ref):
    high_ref[...] = jnp.zeros_like(high_ref)
    total_ref[...] = jnp.zeros_like(total_ref)

    def step(h, carry):
        cols = head(h)
        scores = dot_nt(queries_ref[:, cols], keys_ref[:, cols]) * SCALE
        high = jnp.max(scores, axis=1, keepdims=True)
        weights = jnp.exp2(scores - high).astype(jnp.bfloat16)
        summed = dot(weights, with_ones(values_ref[:, cols]))
        accum_ref[:, cols] = summed[:, :HD]
        put_column(high_ref, h, high)
        put_column(total_ref, h, summed[:, HD : HD + 1])
        return carry

    lax.fori_loop(0, H, step, 0, unroll=2)


def near_kernel(
    coarse_arrays, queries_ref, high_ref, total_ref, accum_ref, mult_ref, near_keys_ref, near_values_ref, *refs
):
    coarse_refs = refs[:coarse_arrays]
    high_out, total_out, accum_out, keys_ref, values_ref, sems = refs[coarse_arrays:]
    width = mult_ref.shape[1]
    odd = lax.rem(lax.axis_index("band"), 2)
    base = pl.multiple_of(odd * width, width)
    copies = [
        pltpu.make_async_copy(near_keys_ref.at[pl.ds(base, width)], keys_ref.at[pl.ds(0, width)], sems.at[0]),
        pltpu.make_async_copy(near_values_ref.at[pl.ds(base, width)], values_ref.at[pl.ds(0, width)], sems.at[1]),
    ]
    count = coarse_refs[0].shape[0] // 2
    for i, ref in enumerate(coarse_refs):
        to = pl.ds(width + i * count, count)
        copies.append(pltpu.make_async_copy(ref.at[pl.ds(0, count)], keys_ref.at[to], sems.at[2 + 2 * i]))
        copies.append(pltpu.make_async_copy(ref.at[pl.ds(count, count)], values_ref.at[to], sems.at[3 + 2 * i]))
    for copy in copies:
        copy.start()
    coarse = keys_ref.shape[0] - width
    bias = jnp.concatenate([log_mult(mult_ref[0:1, :]), jnp.zeros((1, coarse), jnp.float32)], axis=1)
    high_out[...] = jnp.zeros_like(high_out)
    total_out[...] = jnp.zeros_like(total_out)
    for copy in copies:
        copy.wait()

    def step(h, carry):
        cols = head(h)
        scores = dot_nt(queries_ref[:, cols], keys_ref[:, cols]) * SCALE + bias
        old = get_column(high_ref, h)
        high = jnp.maximum(old, jnp.max(scores, axis=1, keepdims=True))
        factor = jnp.exp2(old - high)
        weights = jnp.exp2(scores - high).astype(jnp.bfloat16)
        summed = dot(weights, with_ones(values_ref[:, cols]))
        accum_out[:, cols] = accum_ref[:, cols] * factor + summed[:, :HD]
        put_column(high_out, h, high)
        put_column(total_out, h, get_column(total_ref, h) * factor + summed[:, HD : HD + 1])
        return carry

    lax.fori_loop(0, H, step, 0, unroll=2)


def far_kernel(queries_ref, high_ref, total_ref, accum_ref, far_keys_ref, accum_out, weights_out):
    slots = far_keys_ref.shape[0]
    meta = far_keys_ref[slots - 16 : slots, 0:META_LANES].astype(jnp.float32)
    last = lax.broadcasted_iota(jnp.int32, meta.shape, 0) == 15
    mult = jnp.sum(jnp.where(last, meta, 0.0), axis=0, keepdims=True)
    bias = log_mult(mult[:, 0:slots])

    def step(h, carry):
        cols = head(h)
        scores = dot_nt(queries_ref[:, cols], far_keys_ref[:, cols]) * SCALE + bias
        old = get_column(high_ref, h)
        high = jnp.maximum(old, jnp.max(scores, axis=1, keepdims=True))
        factor = jnp.exp2(old - high)
        weights = jnp.exp2(scores - high)
        total = get_column(total_ref, h) * factor + jnp.sum(weights, axis=1, keepdims=True)
        inverse = 1.0 / total
        accum_out[:, cols] = accum_ref[:, cols] * (factor * inverse)
        weights_out[h] = (weights * inverse).astype(jnp.bfloat16)
        return carry

    lax.fori_loop(0, H, step, 0, unroll=2)


def project_kernel(accum_ref, weights_ref, far_values_ref, gain_ref, matrix_ref, out_ref, normed_ref):
    rows, width = accum_ref.shape
    chunk = 256
    for start in range(0, rows, chunk):
        part = pl.ds(start, chunk)
        heads = [
            accum_ref[part, h * HD : (h + 1) * HD]
            + dot(weights_ref[h, part, :], far_values_ref[:, h * HD : (h + 1) * HD])
            for h in range(H)
        ]
        center = jnp.sum(functools.reduce(jnp.add, heads), axis=1, keepdims=True) * (1.0 / width)
        heads = [x - center for x in heads]
        square = functools.reduce(jnp.add, [x * x for x in heads])
        spread = jnp.sum(square, axis=1, keepdims=True) * (1.0 / width)
        inverse = lax.rsqrt(spread + 1e-05)
        for h, x in enumerate(heads):
            cols = slice(h * HD, (h + 1) * HD)
            normed_ref[part, cols] = (x * inverse * gain_ref[:, cols]).astype(jnp.bfloat16)
        out_ref[part, :] = dot(normed_ref[part, :], matrix_ref[...]).astype(jnp.bfloat16)


def spec(space=VMEM):
    return pl.BlockSpec(memory_space=space)


def call(kernel, ins, outs, scratch=(), limit=24, cost=None):
    flops, nbytes, exps = cost
    return pl.pallas_call(
        kernel,
        in_specs=[spec(s) for _, s in ins],
        out_specs=tuple(spec() for _ in outs),
        out_shape=tuple(
            pltpu.VMEM(shape, dtype) if keep else jax.ShapeDtypeStruct(shape, dtype) for shape, dtype, keep in outs
        ),
        scratch_shapes=list(scratch),
        compiler_params=pltpu.CompilerParams(vmem_limit_bytes=limit << 20),
        cost_estimate=pl.CostEstimate(flops=flops, bytes_accessed=nbytes, transcendentals=exps),
    )(*[x for x, _ in ins])


def on_device(queries, keys, values, out_gain, out_weight, adjacency, send_counts, coarse_index):
    rows, width = queries.shape
    bands = lax.axis_size("band")
    half = adjacency.shape[2]
    count = coarse_index.shape[0]
    slots = half + 16
    bf16, f32 = jnp.bfloat16, jnp.float32
    smem = pltpu.SMEM

    def swap(block, mask):
        return lax.ppermute(block, "band", [(i, i ^ mask) for i in range(bands)])

    def far(block):
        up = [(i, i + 1) for i in range(1, bands - 1, 2)]
        return lax.ppermute(block, "band", up + [(j, i) for i, j in up])

    (coarse,) = call(
        coarse_kernel,
        [(coarse_index.reshape(1, count), VMEM), (keys, VMEM), (values, VMEM)],
        [((2 * count, width), bf16, False)],
        cost=(4 * count * rows * width, 4 * rows * width, 0),
    )
    pieces = [coarse]
    masks = [1] if bands == 2 else [bands - 1] + [1 << i for i in range(bands.bit_length() - 2)]
    for mask in masks:
        pieces = pieces + [swap(piece, mask) for piece in pieces]
    near_keys, near_values = swap(keys, 1), swap(values, 1)
    far_keys, far_values, near_mult = call(
        boundary_kernel,
        [(adjacency, VMEM), (send_counts, smem), (keys, VMEM), (values, VMEM)],
        [((slots, width), bf16, False), ((slots, width), bf16, False), ((8, half), f32, False)],
        cost=(4 * slots * half * width, 4 * rows * width, 0),
    )
    far_keys, far_values = far(far_keys), far(far_values)
    near_mult = swap(near_mult, 1)

    state = [((rows, HD), f32, True), ((rows, HD), f32, True), ((rows, width), f32, True)]
    high, total, accum = call(
        own_kernel,
        [(queries, VMEM), (keys, VMEM), (values, VMEM)],
        state,
        cost=(4 * rows * rows * width, 6 * rows * width, H * rows * rows),
    )
    seen = half + len(pieces) * count
    high, total, accum = call(
        functools.partial(near_kernel, len(pieces)),
        [(queries, VMEM), (high, VMEM), (total, VMEM), (accum, VMEM), (near_mult, VMEM)]
        + [(x, pl.ANY) for x in [near_keys, near_values] + pieces],
        state,
        scratch=[
            pltpu.VMEM((seen, width), bf16),
            pltpu.VMEM((seen, width), bf16),
            pltpu.SemaphoreType.DMA((2 + 2 * len(pieces),)),
        ],
        cost=(4 * rows * seen * width, 2 * rows * width, H * rows * seen),
    )
    accum, weights = call(
        far_kernel,
        [(queries, VMEM), (high, VMEM), (total, VMEM), (accum, VMEM), (far_keys, VMEM)],
        [((rows, width), f32, True), ((H, rows, slots), bf16, True)],
        cost=(2 * rows * slots * width, 2 * rows * width, H * rows * slots),
    )
    (context,) = call(
        project_kernel,
        [
            (accum, VMEM),
            (weights, VMEM),
            (far_values, VMEM),
            (out_gain.reshape(1, width), VMEM),
            (out_weight, VMEM),
        ],
        [((rows, width), bf16, False)],
        scratch=[pltpu.VMEM((rows, width), bf16)],
        cost=(2 * rows * width * (slots + width), 2 * width * width, 0),
    )
    return context


def solution(mesh):
    in_specs = (
        P(("slide", "band"), None),
        P(("slide", "band"), None),
        P(("slide", "band"), None),
        P(),
        P(),
        P(("slide", "band"), None, None),
        P("slide", None),
        P(("slide", "band")),
    )
    out_specs = P(("slide", "band"), None)
    return jax.shard_map(
        on_device, mesh=mesh, in_specs=in_specs, out_specs=out_specs, check_vma=False
    )
```

```python
import functools
import math

import jax
import jax.numpy as jnp
from jax import lax
from jax.experimental import pallas as pl
from jax.experimental.pallas import tpu as pltpu
from jax.sharding import PartitionSpec as P

H = 12
HD = 128
SCALE = math.log2(math.e) / math.sqrt(HD)
DEAD = -1e30
META_LANES = 512

VMEM = pltpu.VMEM
MEMORY = {"any": jax.ShapeDtypeStruct, "vmem": pltpu.VMEM, "hbm": pltpu.HBM, "scalar": jax.ShapeDtypeStruct}
NT = (((1,), (1,)), ((), ()))


def dot(a, b):
    return jnp.dot(a, b, preferred_element_type=jnp.float32)


def dot_nt(a, b):
    return lax.dot_general(a, b, NT, preferred_element_type=jnp.float32)


def column(row):
    n = row.shape[1]
    shape = (n, n)
    diagonal = lax.broadcasted_iota(jnp.int32, shape, 0) == lax.broadcasted_iota(jnp.int32, shape, 1)
    return jnp.sum(jnp.where(diagonal, jnp.broadcast_to(row, shape), 0.0), axis=1, keepdims=True)


def log_mult(mult):
    return jnp.where(mult > 0.0, jnp.log2(jnp.maximum(mult, 1.0)), DEAD)


def coarse_kernel(
    index_hbm, adjacency_hbm, keys_hbm, values_hbm, coarse_ref, near_ref, keys_ref, values_ref, index_ref, adjacency_ref, sems
):
    load_index = pltpu.make_async_copy(index_hbm, index_ref, sems.at[0])
    load_adjacency = pltpu.make_async_copy(adjacency_hbm, adjacency_ref, sems.at[1])
    load_keys = pltpu.make_async_copy(keys_hbm, keys_ref, sems.at[2])
    load_values = pltpu.make_async_copy(values_hbm, values_ref, sems.at[3])
    for load in (load_index, load_adjacency, load_keys, load_values):
        load.start()
    count = index_ref.shape[1]
    rows = keys_ref.shape[0]
    half = adjacency_ref.shape[2]
    side = 1 - lax.rem(lax.axis_index("band"), 2)
    base = pl.multiple_of(side * half, half)
    load_index.wait()
    picked = column(index_ref[...].astype(jnp.float32))
    slots = lax.broadcasted_iota(jnp.int32, (count, rows), 1).astype(jnp.float32)
    choose = (picked == slots).astype(jnp.bfloat16)
    load_adjacency.wait()
    entries = (adjacency_ref[0, pl.ds(side, 1), :] - base).astype(jnp.float32)
    meta = 2 * (half + count)
    near_ref[meta : meta + 16, 0:half] = jnp.broadcast_to(entries, (16, half)).astype(jnp.bfloat16)
    load_keys.wait()
    coarse = dot(choose, keys_ref[...]).astype(jnp.bfloat16)
    coarse_ref[0:count, :] = coarse
    near_ref[2 * half : 2 * half + count, :] = coarse
    near_ref[0:half, :] = keys_ref[pl.ds(base, half), :]
    load_values.wait()
    coarse = dot(choose, values_ref[...]).astype(jnp.bfloat16)
    coarse_ref[count : 2 * count, :] = coarse
    near_ref[2 * half + count : meta, :] = coarse
    near_ref[half : 2 * half, :] = values_ref[pl.ds(base, half), :]


def multiplicity(entries, live):
    width = entries.shape[1]
    shape = (width, width)
    slot = lax.broadcasted_iota(jnp.int32, shape, 0)
    row = lax.broadcasted_iota(jnp.int32, shape, 1).astype(jnp.float32)
    hits = jnp.where((column(entries) == row) & (slot < live), 1.0, 0.0)
    return jnp.sum(hits, axis=0, keepdims=True)


def boundary_kernel(adjacency_ref, counts_ref, keys_ref, values_ref, far_keys_ref, far_values_ref):
    width = adjacency_ref.shape[2]
    slots = far_keys_ref.shape[0]
    band = lax.axis_index("band")
    odd = lax.rem(band, 2)
    base = pl.multiple_of(odd * width, width)
    entries = (adjacency_ref[0, pl.ds(odd, 1), :] - base).astype(jnp.float32)
    mult = multiplicity(entries, counts_ref[odd, band])
    present = (mult > 0.0).astype(jnp.bfloat16)
    square = (width, width)
    before = lax.broadcasted_iota(jnp.int32, square, 0) < lax.broadcasted_iota(jnp.int32, square, 1)
    order = dot(jnp.broadcast_to(present, (16, width)), before.astype(jnp.bfloat16))[0:1, :]
    place = jnp.where(mult > 0.0, order, -1.0)
    wanted = lax.broadcasted_iota(jnp.int32, (slots, width), 0)
    choose = (wanted.astype(jnp.float32) == place) & (wanted < slots - 1)
    choose = jnp.where(choose, 1.0, 0.0).astype(jnp.bfloat16)
    rows = pl.ds(base, width)
    slot_mult = dot_nt(jnp.broadcast_to(mult.astype(jnp.bfloat16), (16, width)), choose)[0:1, :]
    far_keys_ref[...] = dot(choose, keys_ref[rows, :]).astype(jnp.bfloat16)
    distinct = jnp.sum(jnp.where(mult > 0.0, 1.0, 0.0), axis=1, keepdims=True)
    unused = META_LANES - HD - slots
    meta = jnp.concatenate([slot_mult, jnp.zeros((1, unused), jnp.float32), jnp.broadcast_to(distinct, (1, HD))], axis=1)
    tail = slots - 16
    last = lax.broadcasted_iota(jnp.int32, (16, META_LANES), 0) == 15
    old = far_keys_ref[tail:slots, 0:META_LANES].astype(jnp.float32)
    far_keys_ref[tail:slots, 0:META_LANES] = jnp.where(last, meta, old).astype(jnp.bfloat16)
    far_values_ref[...] = dot(choose, values_ref[rows, :]).astype(jnp.bfloat16)


def head(h):
    return slice(h * HD, (h + 1) * HD)


def with_ones(values):
    return jnp.concatenate([values, jnp.ones_like(values)], axis=1)


def own_kernel(queries_ref, keys_ref, values_ref, high_ref, sums_ref):
    for h in range(H):
        cols = head(h)
        scores = dot_nt(queries_ref[:, cols], keys_ref[:, cols]) * SCALE
        high = jnp.max(scores, axis=1, keepdims=True)
        weights = jnp.exp2(scores - high).astype(jnp.bfloat16)
        sums_ref[h] = dot(weights, with_ones(values_ref[:, cols]))
        high_ref[h] = jnp.broadcast_to(high, high_ref.shape[1:])


def near_kernel(counts_ref, queries_ref, high_in, sums_in, near_ref, *refs):
    high_ref, sums_ref = refs[-2:]
    count = refs[0].shape[0] // 2
    half = (near_ref.shape[0] - 16) // 2 - count
    coarse_refs = refs[:-2] + (near_ref.at[2 * half : 2 * half + 2 * count],)
    band = lax.axis_index("band")
    odd = lax.rem(band, 2)
    meta = 2 * (half + count)
    entries = near_ref[meta : meta + 16, 0:half].astype(jnp.float32)[0:1, :]
    bias = log_mult(multiplicity(entries, counts_ref[odd, band + 1 - 2 * odd]))
    for h in range(H):
        cols = head(h)
        queries = queries_ref[:, cols]
        coarse_keys = jnp.concatenate([ref[0:count, cols] for ref in coarse_refs], axis=0)
        coarse_values = jnp.concatenate([ref[count : 2 * count, cols] for ref in coarse_refs], axis=0)
        scores = [
            dot_nt(queries, near_ref[0:half, cols]) * SCALE + bias,
            dot_nt(queries, coarse_keys) * SCALE,
        ]
        old = high_in[h]
        peaks = [jnp.max(x, axis=1, keepdims=True) for x in scores]
        high = jnp.maximum(old, jnp.maximum(peaks[0], peaks[1]))
        factor = jnp.exp2(old - high)
        weights = [jnp.exp2(x - jnp.concatenate([high] * (x.shape[1] // HD), axis=1)) for x in scores]
        weights = jnp.concatenate([x.astype(jnp.bfloat16) for x in weights], axis=1)
        values = jnp.concatenate([near_ref[half : 2 * half, cols], coarse_values], axis=0)
        sums_ref[h] = sums_in[h] * jnp.concatenate([factor, factor], axis=1) + dot(weights, with_ones(values))
        high_ref[h] = high


def far_kernel(queries_ref, high_ref, sums_ref, sent_keys_ref, far_keys_ref, accum_ref, weights_ref, over_ref):
    slots = far_keys_ref.shape[0]
    padded = weights_ref.shape[2]
    pad = padded - slots
    bands = lax.axis_size("band")
    band = lax.axis_index("band")
    edge = (band == 0) | (band == bands - 1)

    def meta_of(ref):
        meta = ref[slots - 16 : slots, 0:META_LANES].astype(jnp.float32)
        last = lax.broadcasted_iota(jnp.int32, meta.shape, 0) == 15
        return jnp.sum(jnp.where(last, meta, 0.0), axis=0, keepdims=True)

    mult = meta_of(far_keys_ref)
    most = jnp.max(jnp.maximum(mult, meta_of(sent_keys_ref))[:, META_LANES - HD :])
    over_ref[0] = jnp.where((most > slots - 1.0) & jnp.logical_not(edge), 1, 0)
    bias = log_mult(jnp.where(edge, 0.0, mult[:, 0:padded]))
    ones = jnp.ones((padded, HD), jnp.bfloat16)
    for h in range(H):
        cols = head(h)
        keys = jnp.concatenate([far_keys_ref[:, cols], jnp.zeros((pad, HD), jnp.bfloat16)], axis=0)
        scores = dot_nt(queries_ref[:, cols], keys) * SCALE + bias
        old = high_ref[h]
        high = jnp.maximum(old, jnp.max(scores, axis=1, keepdims=True))
        factor = jnp.exp2(old - high)
        weights = jnp.exp2(scores - jnp.concatenate([high] * (padded // HD), axis=1))
        total = sums_ref[h, :, HD:] * factor + dot(weights.astype(jnp.bfloat16), ones)
        inverse = 1.0 / total
        accum_ref[:, cols] = sums_ref[h, :, :HD] * (factor * inverse)
        weights_ref[h] = (weights * jnp.concatenate([inverse] * (padded // HD), axis=1)).astype(jnp.bfloat16)


def project_kernel(accum_ref, weights_ref, far_values_ref, gain_ref, matrix_ref, out_ref, normed_ref):
    rows, width = accum_ref.shape
    chunk = 256
    pad = weights_ref.shape[2] - far_values_ref.shape[0]
    for start in range(0, rows, chunk):
        part = pl.ds(start, chunk)
        heads = [
            accum_ref[part, h * HD : (h + 1) * HD]
            + dot(
                weights_ref[h, part, :],
                jnp.concatenate([far_values_ref[:, head(h)], jnp.zeros((pad, HD), jnp.bfloat16)], axis=0),
            )
            for h in range(H)
        ]
        center = jnp.sum(functools.reduce(jnp.add, heads), axis=1, keepdims=True) * (1.0 / width)
        heads = [x - center for x in heads]
        square = functools.reduce(jnp.add, [x * x for x in heads])
        spread = jnp.sum(square, axis=1, keepdims=True) * (1.0 / width)
        inverse = lax.rsqrt(spread + 1e-05)
        for h, x in enumerate(heads):
            cols = slice(h * HD, (h + 1) * HD)
            normed_ref[part, cols] = (x * inverse * gain_ref[:, cols]).astype(jnp.bfloat16)
        out_ref[part, :] = dot(normed_ref[part, :], matrix_ref[...]).astype(jnp.bfloat16)


def spec(space=VMEM):
    return pl.BlockSpec(memory_space=space)


def call(kernel, ins, outs, scratch=(), limit=24, cost=None):
    flops, nbytes, exps = cost
    ins = [(pltpu.with_memory_space_constraint(x, s) if s is pltpu.HBM else x, s) for x, s in ins]
    return pl.pallas_call(
        kernel,
        in_specs=[spec(s) for _, s in ins],
        out_specs=tuple(spec(pltpu.SMEM if keep == "scalar" else VMEM) for _, _, keep in outs),
        out_shape=tuple(
            MEMORY[keep](shape, dtype) for shape, dtype, keep in outs
        ),
        scratch_shapes=list(scratch),
        compiler_params=pltpu.CompilerParams(vmem_limit_bytes=limit << 20),
        cost_estimate=pl.CostEstimate(flops=flops, bytes_accessed=nbytes, transcendentals=exps),
    )(*[x for x, _ in ins])


def on_device(queries, keys, values, out_gain, out_weight, adjacency, send_counts, coarse_index):
    rows, width = queries.shape
    bands = lax.axis_size("band")
    half = adjacency.shape[2]
    count = coarse_index.shape[0]
    slots = half * 11 // 16
    bf16, f32 = jnp.bfloat16, jnp.float32
    smem = pltpu.SMEM

    def swap(block, mask):
        return lax.ppermute(block, "band", [(i, i ^ mask) for i in range(bands)])

    def far(block):
        slides = lax.axis_size("slide")
        pairs = []
        for slide in range(slides):
            for band in range(bands):
                end = band in (0, bands - 1)
                to = (slide ^ 1, band) if end else (slide, band + 1 if band % 2 else band - 1)
                pairs.append((slide * bands + band, to[0] * bands + to[1]))
        return lax.ppermute(block, ("slide", "band"), pairs)

    def across(block):
        up = [(i, i + 1) for i in range(1, bands - 1, 2)]
        return lax.ppermute(block, "band", up + [(j, i) for i, j in up])

    after = lambda first, x: lax.optimization_barrier((first, x))[1]
    resident = ((rows, width), bf16, "vmem")
    coarse, near, keys, values = call(
        coarse_kernel,
        [(x, pltpu.HBM) for x in (coarse_index.reshape(1, count), adjacency, keys, values)],
        [((2 * count, width), bf16, "any"), ((2 * (half + count) + 16, width), bf16, "any"), resident, resident],
        scratch=[
            pltpu.VMEM((1, count), jnp.int32),
            pltpu.VMEM(adjacency.shape, jnp.int32),
            pltpu.SemaphoreType.DMA((4,)),
        ],
        cost=(4 * count * rows * width, 4 * rows * width, 0),
    )
    mirrored = swap(coarse, bands - 1)
    near = swap(near, 1)
    send_counts = send_counts.T

    def boundary(slots):
        return call(
            boundary_kernel,
            [(adjacency, VMEM), (send_counts, smem), (keys, VMEM), (values, VMEM)],
            [((slots, width), bf16, "any"), ((slots, width), bf16, "any")],
            cost=(1, 1, 0),
        )

    def far_weights(sent_keys, far_keys):
        slots = far_keys.shape[0]
        padded = -(-slots // HD) * HD
        return call(
            far_kernel,
            [(queries, VMEM), (high, VMEM), (sums, VMEM), (sent_keys, VMEM), (far_keys, VMEM)],
            [((rows, width), f32, "vmem"), ((H, rows, padded), bf16, "vmem"), ((1,), jnp.int32, "scalar")],
            cost=(2 * rows * slots * width, 2 * rows * width, H * rows * slots),
        )

    def project(accum, weights, far_values):
        operands = (accum, weights, far_values, out_gain.reshape(1, width), out_weight)
        return call(
            project_kernel,
            [(x, VMEM) for x in operands],
            [((rows, width), bf16, "hbm")],
            scratch=[pltpu.VMEM((rows, width), bf16)],
            cost=(2 * rows * width * (half + width), 2 * width * width, 0),
        )[0]

    sent_keys, sent_values = boundary(slots)
    far_keys, far_values = far(sent_keys), far(sent_values)
    own_keys = after(sent_keys, keys)
    high, sums = call(
        own_kernel,
        [(x, VMEM) for x in [queries, own_keys, values]],
        [((H, rows, HD), f32, "vmem"), ((H, rows, 2 * HD), f32, "vmem")],
        cost=(1, 1, 0),
    )
    mirrored = after(high, mirrored)
    pieces = [coarse, mirrored, swap(mirrored, 1)]
    near_piece = near[2 * half : 2 * (half + count)] if bands > 4 else None
    for mask in [1 << i for i in range(1, bands.bit_length() - 2)]:
        pieces = pieces + [swap(piece, mask) for piece in pieces + [near_piece]]

    state = [((H, rows, HD), f32, "vmem"), ((H, rows, 2 * HD), f32, "vmem")]
    seen = half + bands * count
    high, sums = call(
        near_kernel,
        [(send_counts, smem)] + [(x, VMEM) for x in [queries, high, sums, near] + pieces],
        state,
        cost=(7 * rows * seen * width, 2 * rows * width, H * rows * seen),
    )
    accum, weights, over = far_weights(sent_keys, far_keys)

    def all_rows():
        sent_keys, sent_values = boundary(half + 16)
        far_keys, far_values = across(sent_keys), across(sent_values)
        accum, weights, _ = far_weights(sent_keys, far_keys)
        return project(accum, weights, far_values)

    return lax.cond(over[0] > 0, all_rows, lambda: project(accum, weights, far_values))


def solution(mesh):
    in_specs = (
        P(("slide", "band"), None),
        P(("slide", "band"), None),
        P(("slide", "band"), None),
        P(),
        P(),
        P(("slide", "band"), None, None),
        P("slide", None),
        P(("slide", "band")),
    )
    out_specs = P(("slide", "band"), None)
    return jax.shard_map(
        on_device, mesh=mesh, in_specs=in_specs, out_specs=out_specs, check_vma=False
    )
```

```python
import functools
import math

import jax
import jax.numpy as jnp
from jax import lax
from jax.experimental import pallas as pl
from jax.experimental.pallas import tpu as pltpu
from jax.sharding import PartitionSpec as P

H = 12
HD = 128
SCALE = math.log2(math.e) / math.sqrt(HD)
DEAD = -1e30
BLOCKS = 3
GROUPS = 2
META_LANES = 512

VMEM = pltpu.VMEM
MEMORY = {"any": jax.ShapeDtypeStruct, "vmem": pltpu.VMEM, "hbm": pltpu.HBM, "scalar": jax.ShapeDtypeStruct}
SPACE = {"scalar": pltpu.SMEM, "hbm": pltpu.HBM}
NT = (((1,), (1,)), ((), ()))


def dot(a, b):
    return jnp.dot(a, b, preferred_element_type=jnp.float32)


def dot_nt(a, b):
    return lax.dot_general(a, b, NT, preferred_element_type=jnp.float32)


def column(row):
    n = row.shape[1]
    shape = (n, n)
    diagonal = lax.broadcasted_iota(jnp.int32, shape, 0) == lax.broadcasted_iota(jnp.int32, shape, 1)
    return jnp.sum(jnp.where(diagonal, jnp.broadcast_to(row, shape), 0.0), axis=1, keepdims=True)


def log_mult(mult):
    return jnp.where(mult > 0.0, jnp.log2(jnp.maximum(mult, 1.0)), DEAD)


def coarse_kernel(
    index_hbm, adjacency_hbm, keys_hbm, values_hbm, coarse_ref, near_ref, keys_ref, values_ref, index_ref, adjacency_ref, sems
):
    load_index = pltpu.make_async_copy(index_hbm, index_ref, sems.at[0])
    load_adjacency = pltpu.make_async_copy(adjacency_hbm, adjacency_ref, sems.at[1])
    load_keys = pltpu.make_async_copy(keys_hbm, keys_ref, sems.at[2])
    load_values = pltpu.make_async_copy(values_hbm, values_ref, sems.at[3])
    for load in (load_index, load_adjacency, load_keys, load_values):
        load.start()
    count = index_ref.shape[1]
    rows = keys_ref.shape[0]
    half = adjacency_ref.shape[2]
    side = 1 - lax.rem(lax.axis_index("band"), 2)
    base = pl.multiple_of(side * half, half)
    load_index.wait()
    picked = column(index_ref[...].astype(jnp.float32))
    slots = lax.broadcasted_iota(jnp.int32, (count, rows), 1).astype(jnp.float32)
    choose = (picked == slots).astype(jnp.bfloat16)
    load_adjacency.wait()
    entries = (adjacency_ref[0, pl.ds(side, 1), :] - base).astype(jnp.float32)
    meta = 2 * (half + count)
    near_ref[meta : meta + 16, 0:half] = jnp.broadcast_to(entries, (16, half)).astype(jnp.bfloat16)
    load_keys.wait()
    coarse = dot(choose, keys_ref[...]).astype(jnp.bfloat16)
    coarse_ref[0:count, :] = coarse
    near_ref[2 * half : 2 * half + count, :] = coarse
    near_ref[0:half, :] = keys_ref[pl.ds(base, half), :]
    load_values.wait()
    coarse = dot(choose, values_ref[...]).astype(jnp.bfloat16)
    coarse_ref[count : 2 * count, :] = coarse
    near_ref[2 * half + count : meta, :] = coarse
    near_ref[half : 2 * half, :] = values_ref[pl.ds(base, half), :]


def multiplicity(entries, live):
    width = entries.shape[1]
    shape = (width, width)
    slot = lax.broadcasted_iota(jnp.int32, shape, 0)
    row = lax.broadcasted_iota(jnp.int32, shape, 1).astype(jnp.float32)
    hits = jnp.where((column(entries) == row) & (slot < live), 1.0, 0.0)
    return jnp.sum(hits, axis=0, keepdims=True)


def boundary_kernel(adjacency_ref, counts_ref, keys_ref, values_ref, far_keys_ref, far_values_ref):
    width = adjacency_ref.shape[2]
    slots = far_keys_ref.shape[0]
    band = lax.axis_index("band")
    odd = lax.rem(band, 2)
    base = pl.multiple_of(odd * width, width)
    entries = (adjacency_ref[0, pl.ds(odd, 1), :] - base).astype(jnp.float32)
    mult = multiplicity(entries, counts_ref[odd, band])
    present = (mult > 0.0).astype(jnp.bfloat16)
    square = (width, width)
    before = lax.broadcasted_iota(jnp.int32, square, 0) < lax.broadcasted_iota(jnp.int32, square, 1)
    order = dot(jnp.broadcast_to(present, (16, width)), before.astype(jnp.bfloat16))[0:1, :]
    place = jnp.where(mult > 0.0, order, -1.0)
    wanted = lax.broadcasted_iota(jnp.int32, (slots, width), 0)
    choose = (wanted.astype(jnp.float32) == place) & (wanted < slots - 1)
    choose = jnp.where(choose, 1.0, 0.0).astype(jnp.bfloat16)
    rows = pl.ds(base, width)
    slot_mult = dot_nt(jnp.broadcast_to(mult.astype(jnp.bfloat16), (16, width)), choose)[0:1, :]
    far_keys_ref[...] = dot(choose, keys_ref[rows, :]).astype(jnp.bfloat16)
    distinct = jnp.sum(jnp.where(mult > 0.0, 1.0, 0.0), axis=1, keepdims=True)
    unused = META_LANES - HD - slots
    meta = jnp.concatenate([slot_mult, jnp.zeros((1, unused), jnp.float32), jnp.broadcast_to(distinct, (1, HD))], axis=1)
    tail = slots - 16
    last = lax.broadcasted_iota(jnp.int32, (16, META_LANES), 0) == 15
    old = far_keys_ref[tail:slots, 0:META_LANES].astype(jnp.float32)
    far_keys_ref[tail:slots, 0:META_LANES] = jnp.where(last, meta, old).astype(jnp.bfloat16)
    far_values_ref[...] = dot(choose, values_ref[rows, :]).astype(jnp.bfloat16)


def head(h):
    return slice(h * HD, (h + 1) * HD)


def tiles(x):
    return [x[:, i : i + HD] for i in range(0, x.shape[1], HD)]


def across_tiles(slab, columns):
    return jnp.concatenate([slab] * (columns // HD), axis=1)


def with_ones(values):
    return jnp.concatenate([values, jnp.ones_like(values)], axis=1)


def near_kernel(half, first, counts_ref, queries_ref, keys_ref, values_ref, near_ref, high_ref, sums_ref):
    band = lax.axis_index("band")
    odd = lax.rem(band, 2)
    entries = near_ref[near_ref.shape[0] - 16 :, 0:half].astype(jnp.float32)[0:1, :]
    bias = log_mult(multiplicity(entries, counts_ref[odd, band + 1 - 2 * odd]))
    for h in range(high_ref.shape[0]):
        cols = head(first + h)
        queries = queries_ref[:, cols]
        scores = [
            dot_nt(queries, keys_ref[:, cols]) * SCALE,
            dot_nt(queries, near_ref[0:half, cols]) * SCALE + bias,
        ]
        high = jnp.maximum(*[jnp.max(x, axis=1, keepdims=True) for x in scores])
        weights = jnp.concatenate([jnp.exp2(x - high).astype(jnp.bfloat16) for x in scores], axis=1)
        values = jnp.concatenate([values_ref[:, cols], near_ref[half : 2 * half, cols]], axis=0)
        sums_ref[h] = dot(weights, with_ones(values))
        high_ref[h] = jnp.broadcast_to(high, high_ref.shape[1:])


def far_kernel(exact, groups, queries_ref, sent_keys_ref, far_keys_ref, near_ref, *refs):
    states, (accum_ref, weights_ref, state_ref) = refs[: 2 * groups], refs[-3:]
    coarse_refs = refs[2 * groups : -3]
    coarse = coarse_refs[0].shape[0]
    count = coarse // 2
    end = near_ref.shape[0] - 16
    coarse_refs += (near_ref.at[end - coarse : end],)
    rows = queries_ref.shape[0]
    slots = far_keys_ref.shape[0]
    padded = weights_ref.shape[2]
    pad = padded - slots
    bands = lax.axis_size("band")
    band = lax.axis_index("band")
    edge = (band == 0) | (band == bands - 1)

    def meta_of(ref):
        meta = ref[slots - 16 : slots, 0:META_LANES].astype(jnp.float32)
        last = lax.broadcasted_iota(jnp.int32, meta.shape, 0) == 15
        return jnp.sum(jnp.where(last, meta, 0.0), axis=0, keepdims=True)

    mult = meta_of(far_keys_ref)
    most = jnp.max(jnp.maximum(mult, meta_of(sent_keys_ref))[:, META_LANES - HD :])
    overflow = (most > slots - 1.0) & jnp.logical_not(edge)
    bias = log_mult(jnp.where(edge, 0.0, mult[:, 0:padded]))
    ones = jnp.ones((padded, HD), jnp.bfloat16)
    all_totals = jnp.zeros((rows, HD), jnp.float32)
    for h in range(H):
        high_ref, sums_ref = states[2 * (h * groups // H) : 2 * (h * groups // H) + 2]
        place = h % (H // groups)
        cols = head(h)
        queries = queries_ref[:, cols]
        keys = jnp.concatenate([far_keys_ref[:, cols], jnp.zeros((pad, HD), jnp.bfloat16)], axis=0)
        coarse_keys = jnp.concatenate([ref[0:count, cols] for ref in coarse_refs], axis=0)
        coarse_values = jnp.concatenate([ref[count:coarse, cols] for ref in coarse_refs], axis=0)
        scores = dot_nt(queries, keys) * SCALE + bias
        coarse_scores = dot_nt(queries, coarse_keys) * SCALE
        high, summed = high_ref[place], sums_ref[place]
        if exact:
            peak = functools.reduce(jnp.maximum, tiles(scores) + tiles(coarse_scores))
            old, high = high, jnp.maximum(high, jnp.max(peak, axis=1, keepdims=True))
            summed = summed * across_tiles(jnp.exp2(old - high), 2 * HD)
        weights = jnp.exp2(scores - across_tiles(high, padded))
        coarse_weights = jnp.exp2(coarse_scores - across_tiles(high, coarse_scores.shape[1])).astype(jnp.bfloat16)
        summed = summed + dot(coarse_weights, with_ones(coarse_values))
        total = summed[:, HD:] + dot(weights.astype(jnp.bfloat16), ones)
        all_totals = all_totals + total
        inverse = 1.0 / total
        accum_ref[:, cols] = summed[:, :HD] * inverse
        weights_ref[h] = (weights * across_tiles(inverse, padded)).astype(jnp.bfloat16)
    safe = jnp.max(all_totals) < 2.0**100
    state_ref[0] = jnp.where(overflow, 2, jnp.where(safe | exact, 0, 1))


def project_kernel(accum_ref, weights_ref, far_values_ref, gain_ref, matrix_ref, out_hbm, normed_ref, out_ref, sems):
    rows, width = accum_ref.shape
    pad = weights_ref.shape[2] - far_values_ref.shape[0]
    chunk = 256
    for start in range(0, rows, chunk):
        part = pl.ds(start, chunk)
        heads = [
            accum_ref[part, head(h)]
            + dot(
                weights_ref[h, part, :],
                jnp.concatenate([far_values_ref[:, head(h)], jnp.zeros((pad, HD), jnp.bfloat16)], axis=0),
            )
            for h in range(H)
        ]
        center = jnp.sum(functools.reduce(jnp.add, heads), axis=1, keepdims=True) * (1.0 / width)
        heads = [x - center for x in heads]
        square = functools.reduce(jnp.add, [x * x for x in heads])
        spread = jnp.sum(square, axis=1, keepdims=True) * (1.0 / width)
        inverse = lax.rsqrt(spread + 1e-05)
        for h, x in enumerate(heads):
            normed_ref[part, head(h)] = (x * inverse * gain_ref[:, head(h)]).astype(jnp.bfloat16)
    block = width // BLOCKS
    copies = []
    for i in range(BLOCKS):
        cols = pl.ds(i * block, block)
        out_ref[:, cols] = dot(normed_ref[...], matrix_ref[:, cols]).astype(jnp.bfloat16)
        copies.append(pltpu.make_async_copy(out_ref.at[:, cols], out_hbm.at[:, cols], sems.at[i]))
        copies[-1].start()
    for copy in copies:
        copy.wait()


def spec(space=VMEM):
    return pl.BlockSpec(memory_space=space)


def call(kernel, ins, outs, scratch=(), limit=24, cost=None):
    flops, nbytes, exps = cost
    ins = [(pltpu.with_memory_space_constraint(x, s) if s is pltpu.HBM else x, s) for x, s in ins]
    return pl.pallas_call(
        kernel,
        in_specs=[spec(s) for _, s in ins],
        out_specs=tuple(spec(SPACE.get(keep, VMEM)) for _, _, keep in outs),
        out_shape=tuple(
            MEMORY[keep](shape, dtype) for shape, dtype, keep in outs
        ),
        scratch_shapes=list(scratch),
        compiler_params=pltpu.CompilerParams(vmem_limit_bytes=limit << 20),
        cost_estimate=pl.CostEstimate(flops=flops, bytes_accessed=nbytes, transcendentals=exps),
    )(*[x for x, _ in ins])


def on_device(queries, keys, values, out_gain, out_weight, adjacency, send_counts, coarse_index):
    rows, width = queries.shape
    bands = lax.axis_size("band")
    half = adjacency.shape[2]
    count = coarse_index.shape[0]
    slots = half * 11 // 16
    bf16, f32 = jnp.bfloat16, jnp.float32
    smem = pltpu.SMEM

    def swap(block, mask):
        return lax.ppermute(block, "band", [(i, i ^ mask) for i in range(bands)])

    def far(block):
        slides = lax.axis_size("slide")
        pairs = []
        for slide in range(slides):
            for band in range(bands):
                end = band in (0, bands - 1)
                to = (slide ^ 1, band) if end else (slide, band + 1 if band % 2 else band - 1)
                pairs.append((slide * bands + band, to[0] * bands + to[1]))
        return lax.ppermute(block, ("slide", "band"), pairs)

    def across(block):
        up = [(i, i + 1) for i in range(1, bands - 1, 2)]
        return lax.ppermute(block, "band", up + [(j, i) for i, j in up])

    after = lambda first, x: lax.optimization_barrier((first, x))[1]
    resident = ((rows, width), bf16, "vmem")
    coarse, near, keys, values = call(
        coarse_kernel,
        [(x, pltpu.HBM) for x in (coarse_index.reshape(1, count), adjacency, keys, values)],
        [((2 * count, width), bf16, "any"), ((2 * (half + count) + 16, width), bf16, "any"), resident, resident],
        scratch=[
            pltpu.VMEM((1, count), jnp.int32),
            pltpu.VMEM(adjacency.shape, jnp.int32),
            pltpu.SemaphoreType.DMA((4,)),
        ],
        cost=(4 * count * rows * width, 4 * rows * width, 0),
    )
    mirrored = swap(coarse, bands - 1)
    near = swap(near, 1)
    send_counts = send_counts.T

    def boundary(slots):
        return call(
            boundary_kernel,
            [(adjacency, VMEM), (send_counts, smem), (keys, VMEM), (values, VMEM)],
            [((slots, width), bf16, "any"), ((slots, width), bf16, "any")],
            cost=(1, 1, 0),
        )

    def far_weights(exact, states, sent_keys, far_keys):
        slots = far_keys.shape[0]
        padded = -(-slots // HD) * HD
        return call(
            functools.partial(far_kernel, exact, len(states)),
            [(x, VMEM) for x in [queries, sent_keys, far_keys, near] + sum(states, []) + pieces],
            [((rows, width), f32, "vmem"), ((H, rows, padded), bf16, "vmem"), ((1,), jnp.int32, "scalar")],
            cost=(4 * rows * slots * width, 2 * rows * width, H * rows * slots),
        )

    def project(accum, weights, far_values):
        operands = (accum, weights, far_values, gain, out_weight)
        return call(
            project_kernel,
            [(x, VMEM) for x in operands],
            [((rows, width), bf16, "hbm")],
            scratch=[pltpu.VMEM((rows, width), bf16)] * 2 + [pltpu.SemaphoreType.DMA((BLOCKS,))],
            cost=(2 * rows * width * (half + width), 2 * width * width, 0),
        )[0]

    sent_keys, sent_values = boundary(slots)
    far_values = far(sent_values)
    far_keys = far(sent_keys)
    own_keys = after(sent_keys, keys)
    states = []
    for group in range(GROUPS):
        heads = H // GROUPS
        high, sums = call(
            functools.partial(near_kernel, half, group * heads),
            [(send_counts, smem)] + [(x, VMEM) for x in [queries, own_keys, values, near]],
            [((heads, rows, HD), f32, "vmem"), ((heads, rows, 2 * HD), f32, "vmem")],
            cost=(22 * group * rows * half * width, 2, 0),
        )
        states.append([high, sums])
        if group == 0:
            mirrored = after(high, mirrored)
            own_keys = after(mirrored, own_keys)
    pieces = [coarse, mirrored, swap(mirrored, 1)]
    near_piece = near[2 * half : 2 * (half + count)] if bands > 4 else None
    for mask in [1 << i for i in range(1, bands.bit_length() - 2)]:
        pieces = pieces + [swap(piece, mask) for piece in pieces + [near_piece]]
    accum, weights, state = far_weights(False, states, sent_keys, far_keys)
    gain = after(accum, out_gain.reshape(1, width))

    def exact():
        accum, weights, _ = far_weights(True, states, sent_keys, far_keys)
        return project(accum, weights, far_values)

    def all_rows():
        sent_keys, sent_values = boundary(half + 16)
        far_keys, far_values = across(sent_keys), across(sent_values)
        accum, weights, _ = far_weights(True, states, sent_keys, far_keys)
        return project(accum, weights, far_values)

    return lax.switch(state[0], [lambda: project(accum, weights, far_values), exact, all_rows])


def solution(mesh):
    in_specs = (
        P(("slide", "band"), None),
        P(("slide", "band"), None),
        P(("slide", "band"), None),
        P(),
        P(),
        P(("slide", "band"), None, None),
        P("slide", None),
        P(("slide", "band")),
    )
    out_specs = P(("slide", "band"), None)
    return jax.shard_map(
        on_device, mesh=mesh, in_specs=in_specs, out_specs=out_specs, check_vma=False
    )
```

```python
import functools
import math

import jax
import jax.numpy as jnp
from jax import lax
from jax.experimental import pallas as pl
from jax.experimental.pallas import tpu as pltpu
from jax.sharding import PartitionSpec as P

H = 12
HD = 128
SCALE = math.log2(math.e) / math.sqrt(HD)
DEAD = -1e30
BLOCKS = 3
COARSE_LANE = 384
COUNT_LANE = 512
META_LANES = 640

VMEM = pltpu.VMEM
MEMORY = {"any": jax.ShapeDtypeStruct, "vmem": pltpu.VMEM, "hbm": pltpu.HBM, "scalar": jax.ShapeDtypeStruct}
SPACE = {"scalar": pltpu.SMEM, "hbm": pltpu.HBM}
NT = (((1,), (1,)), ((), ()))


def dot(a, b):
    return jnp.dot(a, b, preferred_element_type=jnp.float32)


def dot_nt(a, b):
    return lax.dot_general(a, b, NT, preferred_element_type=jnp.float32)


def column(row):
    n = row.shape[1]
    shape = (n, n)
    diagonal = lax.broadcasted_iota(jnp.int32, shape, 0) == lax.broadcasted_iota(jnp.int32, shape, 1)
    return jnp.sum(jnp.where(diagonal, jnp.broadcast_to(row, shape), 0.0), axis=1, keepdims=True)


def log_mult(mult):
    return jnp.where(mult > 0.0, jnp.log2(jnp.maximum(mult, 1.0)), DEAD)


def coarse_kernel(
    index_hbm, adjacency_hbm, keys_hbm, values_hbm, coarse_ref, near_ref, keys_ref, values_ref, index_ref, adjacency_ref, sems
):
    load_index = pltpu.make_async_copy(index_hbm, index_ref, sems.at[0])
    load_adjacency = pltpu.make_async_copy(adjacency_hbm, adjacency_ref, sems.at[1])
    load_keys = pltpu.make_async_copy(keys_hbm, keys_ref, sems.at[2])
    load_values = pltpu.make_async_copy(values_hbm, values_ref, sems.at[3])
    for load in (load_index, load_adjacency, load_keys, load_values):
        load.start()
    count = index_ref.shape[1]
    rows = keys_ref.shape[0]
    half = adjacency_ref.shape[2]
    side = 1 - lax.rem(lax.axis_index("band"), 2)
    base = pl.multiple_of(side * half, half)
    load_index.wait()
    picked = column(index_ref[...].astype(jnp.float32))
    slots = lax.broadcasted_iota(jnp.int32, (count, rows), 1).astype(jnp.float32)
    choose = (picked == slots).astype(jnp.bfloat16)
    load_adjacency.wait()
    entries = (adjacency_ref[0, pl.ds(side, 1), :] - base).astype(jnp.float32)
    meta = 2 * (half + count)
    near_ref[meta : meta + 16, 0:half] = jnp.broadcast_to(entries, (16, half)).astype(jnp.bfloat16)
    load_keys.wait()
    coarse = dot(choose, keys_ref[...]).astype(jnp.bfloat16)
    coarse_ref[0:count, :] = coarse
    near_ref[2 * half : 2 * half + count, :] = coarse
    near_ref[0:half, :] = keys_ref[pl.ds(base, half), :]
    load_values.wait()
    coarse = dot(choose, values_ref[...]).astype(jnp.bfloat16)
    coarse_ref[count : 2 * count, :] = coarse
    near_ref[2 * half + count : meta, :] = coarse
    near_ref[half : 2 * half, :] = values_ref[pl.ds(base, half), :]


def multiplicity(entries, live):
    width = entries.shape[1]
    shape = (width, width)
    slot = lax.broadcasted_iota(jnp.int32, shape, 0)
    row = lax.broadcasted_iota(jnp.int32, shape, 1).astype(jnp.float32)
    hits = jnp.where((column(entries) == row) & (slot < live), 1.0, 0.0)
    return jnp.sum(hits, axis=0, keepdims=True)


def boundary_kernel(
    apart, index_ref, adjacency_ref, counts_ref, keys_ref, values_ref, far_keys_ref, far_values_ref
):
    width = adjacency_ref.shape[2]
    slots = far_keys_ref.shape[0]
    count = index_ref.shape[1]
    band = lax.axis_index("band")
    odd = lax.rem(band, 2)
    base = pl.multiple_of(odd * width, width)
    entries = (adjacency_ref[0, pl.ds(odd, 1), :] - base).astype(jnp.float32)
    mult = multiplicity(entries, counts_ref[odd, band])
    coarse = column((index_ref[...] - base).astype(jnp.float32))
    coarse = coarse == lax.broadcasted_iota(jnp.int32, (count, width), 1).astype(jnp.float32)
    coarse = jnp.where(coarse, 1.0 if apart else 0.0, 0.0)
    coarse_mult = dot_nt(jnp.broadcast_to(mult.astype(jnp.bfloat16), (16, width)), coarse.astype(jnp.bfloat16))[0:1, :]
    mult = jnp.where(jnp.sum(coarse, axis=0, keepdims=True) > 0.0, 0.0, mult)
    present = (mult > 0.0).astype(jnp.bfloat16)
    square = (width, width)
    before = lax.broadcasted_iota(jnp.int32, square, 0) < lax.broadcasted_iota(jnp.int32, square, 1)
    order = dot(jnp.broadcast_to(present, (16, width)), before.astype(jnp.bfloat16))[0:1, :]
    place = jnp.where(mult > 0.0, order + 1.0, -1.0)
    wanted = lax.broadcasted_iota(jnp.int32, (slots, width), 0)
    choose = jnp.where(wanted.astype(jnp.float32) == place, 1.0, 0.0).astype(jnp.bfloat16)
    rows = pl.ds(base, width)
    slot_mult = dot_nt(jnp.broadcast_to(mult.astype(jnp.bfloat16), (16, width)), choose)[0:1, :]
    far_keys_ref[...] = dot(choose, keys_ref[rows, :]).astype(jnp.bfloat16)
    distinct = jnp.sum(jnp.where(mult > 0.0, 1.0, 0.0), axis=1, keepdims=True)
    pieces = [slot_mult, coarse_mult, jnp.broadcast_to(distinct, (1, META_LANES - COUNT_LANE))]
    starts = [0, COARSE_LANE, COUNT_LANE, META_LANES]
    padded = [
        jnp.concatenate([x, jnp.zeros((1, end - start - x.shape[1]), jnp.float32)], axis=1)
        if end - start > x.shape[1]
        else x
        for x, start, end in zip(pieces, starts, starts[1:])
    ]
    meta = jnp.concatenate(padded, axis=1)
    first = lax.broadcasted_iota(jnp.int32, (16, META_LANES), 0) == 0
    old = far_keys_ref[0:16, 0:META_LANES].astype(jnp.float32)
    far_keys_ref[0:16, 0:META_LANES] = jnp.where(first, meta, old).astype(jnp.bfloat16)
    far_values_ref[...] = dot(choose, values_ref[rows, :]).astype(jnp.bfloat16)


def head(h):
    return slice(h * HD, (h + 1) * HD)


def tiles(x):
    return [x[:, i : i + HD] for i in range(0, x.shape[1], HD)]


def across_tiles(slab, columns):
    return jnp.concatenate([slab] * (columns // HD), axis=1)


def with_ones(values):
    return jnp.concatenate([values, jnp.ones_like(values)], axis=1)


def near_kernel(exact, half, first, counts_ref, queries_ref, keys_ref, values_ref, near_ref, sums_ref, *high_ref):
    band = lax.axis_index("band")
    odd = lax.rem(band, 2)
    entries = near_ref[near_ref.shape[0] - 16 :, 0:half].astype(jnp.float32)[0:1, :]
    bias = log_mult(multiplicity(entries, counts_ref[odd, band + 1 - 2 * odd]))
    for h in range(sums_ref.shape[0]):
        cols = head(first + h)
        queries = queries_ref[:, cols]
        scores = [
            dot_nt(queries, keys_ref[:, cols]) * SCALE,
            dot_nt(queries, near_ref[0:half, cols]) * SCALE + bias,
        ]
        if exact:
            high = jnp.maximum(*[jnp.max(x, axis=1, keepdims=True) for x in scores])
            scores = [x - high for x in scores]
            high_ref[0][h] = jnp.broadcast_to(high, high_ref[0].shape[1:])
        weights = jnp.concatenate([jnp.exp2(x).astype(jnp.bfloat16) for x in scores], axis=1)
        values = jnp.concatenate([values_ref[:, cols], near_ref[half : 2 * half, cols]], axis=0)
        sums_ref[h] = dot(weights, with_ones(values))


def far_kernel(exact, groups, queries_ref, sent_keys_ref, far_keys_ref, near_ref, *refs):
    sums_refs, (accum_ref, weights_ref, state_ref, keys_ref) = refs[:groups], refs[-4:]
    high_ref = refs[groups] if exact else None
    coarse_refs = refs[groups + exact : -4]
    coarse = coarse_refs[0].shape[0]
    count = coarse // 2
    end = near_ref.shape[0] - 16
    coarse_refs += (near_ref.at[end - coarse : end],)
    rows = queries_ref.shape[0]
    slots = far_keys_ref.shape[0]
    padded = weights_ref.shape[2]
    bands = lax.axis_size("band")
    band = lax.axis_index("band")
    edge = (band == 0) | (band == bands - 1)

    def meta_of(ref):
        meta = ref[0:16, 0:META_LANES].astype(jnp.float32)
        first = lax.broadcasted_iota(jnp.int32, meta.shape, 0) == 0
        return jnp.sum(jnp.where(first, meta, 0.0), axis=0, keepdims=True)

    keys_ref[slots // 16 * 16 : padded, :] = jnp.zeros((padded - slots // 16 * 16, keys_ref.shape[1]), jnp.bfloat16)
    keys_ref[0:slots, :] = far_keys_ref[...]
    mult = jnp.where(edge, 0.0, meta_of(far_keys_ref))
    most = jnp.max(jnp.maximum(mult, meta_of(sent_keys_ref))[:, COUNT_LANE:])
    overflow = (most > slots - 1.0) & jnp.logical_not(edge)
    bias = log_mult(mult[:, 0:padded])
    coarse_mult = mult[:, COARSE_LANE : COARSE_LANE + count]
    others = jnp.zeros((1, len(coarse_refs) * count - 2 * count), jnp.float32)
    coarse_bias = jnp.concatenate([jnp.zeros((1, count), jnp.float32), jnp.log2(1.0 + coarse_mult), others], axis=1)
    ones = jnp.ones((padded, HD), jnp.bfloat16)
    sizes = jnp.zeros((rows, HD), jnp.float32)
    for h in range(H):
        summed = sums_refs[h * groups // H][h % (H // groups)]
        cols = head(h)
        queries = queries_ref[:, cols]
        coarse_keys = jnp.concatenate([ref[0:count, cols] for ref in coarse_refs], axis=0)
        coarse_values = jnp.concatenate([ref[count:coarse, cols] for ref in coarse_refs], axis=0)
        scores = dot_nt(queries, keys_ref[:, cols]) * SCALE + bias
        coarse_scores = dot_nt(queries, coarse_keys) * SCALE + coarse_bias
        if exact:
            old = high_ref[h]
            peak = functools.reduce(jnp.maximum, tiles(scores) + tiles(coarse_scores))
            high = jnp.maximum(old, jnp.max(peak, axis=1, keepdims=True))
            summed = summed * across_tiles(jnp.exp2(old - high), 2 * HD)
            scores = scores - across_tiles(high, padded)
            coarse_scores = coarse_scores - across_tiles(high, coarse_scores.shape[1])
        weights = jnp.exp2(scores)
        coarse_weights = jnp.exp2(coarse_scores).astype(jnp.bfloat16)
        summed = summed + dot(coarse_weights, with_ones(coarse_values))
        total = summed[:, HD:] + dot(weights.astype(jnp.bfloat16), ones)
        inverse = 1.0 / total
        sizes = sizes + (total + inverse)
        accum_ref[:, cols] = summed[:, :HD] * inverse
        weights_ref[h] = (weights * across_tiles(inverse, padded)).astype(jnp.bfloat16)
    safe = jnp.max(sizes) < 2.0**60
    state_ref[0] = jnp.where(overflow, 2, jnp.where(safe | exact, 0, 1))


def project_kernel(accum_ref, weights_ref, far_values_ref, gain_ref, matrix_ref, out_hbm, normed_ref, out_ref, values_ref, sems):
    rows, width = accum_ref.shape
    slots, padded = far_values_ref.shape[0], values_ref.shape[0]
    values_ref[slots // 16 * 16 : padded, :] = jnp.zeros((padded - slots // 16 * 16, width), jnp.bfloat16)
    values_ref[0:slots, :] = far_values_ref[...]
    chunk = 256
    for start in range(0, rows, chunk):
        part = pl.ds(start, chunk)
        heads = [
            accum_ref[part, head(h)]
            + dot(weights_ref[h, part, :], values_ref[:, head(h)])
            for h in range(H)
        ]
        center = jnp.sum(functools.reduce(jnp.add, heads), axis=1, keepdims=True) * (1.0 / width)
        heads = [x - center for x in heads]
        square = functools.reduce(jnp.add, [x * x for x in heads])
        spread = jnp.sum(square, axis=1, keepdims=True) * (1.0 / width)
        inverse = lax.rsqrt(spread + 1e-05)
        for h, x in enumerate(heads):
            normed_ref[part, head(h)] = (x * inverse * gain_ref[:, head(h)]).astype(jnp.bfloat16)
    block = width // BLOCKS
    copies = []
    for i in range(BLOCKS):
        cols = pl.ds(i * block, block)
        out_ref[:, cols] = dot(normed_ref[...], matrix_ref[:, cols]).astype(jnp.bfloat16)
        copies.append(pltpu.make_async_copy(out_ref.at[:, cols], out_hbm.at[:, cols], sems.at[i]))
        copies[-1].start()
    for copy in copies:
        copy.wait()


def spec(space=VMEM):
    return pl.BlockSpec(memory_space=space)


def call(kernel, ins, outs, scratch=(), limit=24, cost=None):
    flops, nbytes, exps = cost
    ins = [(pltpu.with_memory_space_constraint(x, s) if s is pltpu.HBM else x, s) for x, s in ins]
    return pl.pallas_call(
        kernel,
        in_specs=[spec(s) for _, s in ins],
        out_specs=tuple(spec(SPACE.get(keep, VMEM)) for _, _, keep in outs),
        out_shape=tuple(
            MEMORY[keep](shape, dtype) for shape, dtype, keep in outs
        ),
        scratch_shapes=list(scratch),
        compiler_params=pltpu.CompilerParams(vmem_limit_bytes=limit << 20),
        cost_estimate=pl.CostEstimate(flops=flops, bytes_accessed=nbytes, transcendentals=exps),
    )(*[x for x, _ in ins])


def on_device(queries, keys, values, out_gain, out_weight, adjacency, send_counts, coarse_index):
    rows, width = queries.shape
    bands = lax.axis_size("band")
    half = adjacency.shape[2]
    count = coarse_index.shape[0]
    slots = (half * 21 // 32 if bands == 4 else half * 11 // 16) // 8 * 8
    bf16, f32 = jnp.bfloat16, jnp.float32
    smem = pltpu.SMEM

    def swap(block, mask):
        return lax.ppermute(block, "band", [(i, i ^ mask) for i in range(bands)])

    def far(block):
        slides = lax.axis_size("slide")
        pairs = []
        for slide in range(slides):
            for band in range(bands):
                end = band in (0, bands - 1)
                to = (slide ^ 1, band) if end else (slide, band + 1 if band % 2 else band - 1)
                pairs.append((slide * bands + band, to[0] * bands + to[1]))
        return lax.ppermute(block, ("slide", "band"), pairs)

    def across(block):
        up = [(i, i + 1) for i in range(1, bands - 1, 2)]
        return lax.ppermute(block, "band", up + [(j, i) for i, j in up])

    index = coarse_index.reshape(1, count)
    after = lambda first, x: lax.optimization_barrier((first, x))[1]
    resident = ((rows, width), bf16, "vmem")
    coarse, near, keys, values = call(
        coarse_kernel,
        [(x, pltpu.HBM) for x in (index, adjacency, keys, values)],
        [((2 * count, width), bf16, "any"), ((2 * (half + count) + 16, width), bf16, "any"), resident, resident],
        scratch=[
            pltpu.VMEM((1, count), jnp.int32),
            pltpu.VMEM(adjacency.shape, jnp.int32),
            pltpu.SemaphoreType.DMA((4,)),
        ],
        cost=(4 * count * rows * width, 4 * rows * width, 0),
    )
    mirrored = swap(coarse, bands - 1)
    near = swap(near, 1)
    send_counts = send_counts.T

    def boundary(slots):
        return call(
            functools.partial(boundary_kernel, bands == 4),
            [(index, VMEM), (adjacency, VMEM), (send_counts, smem), (keys, VMEM), (values, VMEM)],
            [((slots, width), bf16, "any"), ((slots, width), bf16, "any")],
            cost=(1, 1, 0),
        )

    def near_sums(exact, keys, first, heads):
        wide = ((heads, rows, 2 * HD), f32, "vmem")
        return call(
            functools.partial(near_kernel, exact, half, first),
            [(send_counts, smem)] + [(x, VMEM) for x in [queries, keys, values, near]],
            [wide, ((heads, rows, HD), f32, "vmem")] if exact else [wide],
            cost=((21 if first else 0) * rows * half * width, 2, 0),
        )

    def far_weights(exact, states, sent_keys, far_keys):
        slots = far_keys.shape[0]
        padded = -(-slots // HD) * HD
        return call(
            functools.partial(far_kernel, exact, len(states) - exact),
            [(x, VMEM) for x in [queries, sent_keys, far_keys, near] + list(states) + pieces],
            [((rows, width), f32, "vmem"), ((H, rows, padded), bf16, "vmem"), ((1,), jnp.int32, "scalar")],
            scratch=[pltpu.VMEM((padded, width), bf16)],
            cost=(4 * rows * slots * width, 2 * rows * width, H * rows * slots),
        )

    def project(accum, weights, far_values):
        operands = (accum, weights, far_values, gain, out_weight)
        return call(
            project_kernel,
            [(x, VMEM) for x in operands],
            [((rows, width), bf16, "hbm")],
            scratch=[
                pltpu.VMEM((rows, width), bf16),
                pltpu.VMEM((rows, width), bf16),
                pltpu.VMEM((weights.shape[2], width), bf16),
                pltpu.SemaphoreType.DMA((BLOCKS,)),
            ],
            cost=(2 * rows * width * (half + width), 2 * width * width, 0),
        )[0]

    sent_keys, sent_values = boundary(slots)
    far_keys, far_values = far(sent_keys), far(sent_values)
    own_keys = after(sent_keys, keys)
    half_heads = H // 2
    (first,) = near_sums(False, own_keys, 0, half_heads)
    mirrored = after(first, mirrored)
    (second,) = near_sums(False, after(mirrored, own_keys), half_heads, H - half_heads)
    states = [first, second]
    pieces = [coarse, mirrored, swap(mirrored, 1)]
    near_piece = near[2 * half : 2 * (half + count)] if bands > 4 else None
    for mask in [1 << i for i in range(1, bands.bit_length() - 2)]:
        pieces = pieces + [swap(piece, mask) for piece in pieces + [near_piece]]
    accum, weights, state = far_weights(False, states, sent_keys, far_keys)
    gain = after(accum, out_gain.reshape(1, width))

    def exact():
        accum, weights, _ = far_weights(True, near_sums(True, keys, 0, H), sent_keys, far_keys)
        return project(accum, weights, far_values)

    def all_rows():
        sent_keys, sent_values = boundary(half + 16)
        far_keys, far_values = across(sent_keys), across(sent_values)
        accum, weights, _ = far_weights(True, near_sums(True, keys, 0, H), sent_keys, far_keys)
        return project(accum, weights, far_values)

    return lax.switch(state[0], [lambda: project(accum, weights, far_values), exact, all_rows])


def solution(mesh):
    in_specs = (
        P(("slide", "band"), None),
        P(("slide", "band"), None),
        P(("slide", "band"), None),
        P(),
        P(),
        P(("slide", "band"), None, None),
        P("slide", None),
        P(("slide", "band")),
    )
    out_specs = P(("slide", "band"), None)
    return jax.shard_map(
        on_device, mesh=mesh, in_specs=in_specs, out_specs=out_specs, check_vma=False
    )
```

```python
import functools
import math

import jax
import jax.numpy as jnp
from jax import lax
from jax.experimental import pallas as pl
from jax.experimental.pallas import tpu as pltpu
from jax.sharding import PartitionSpec as P

H = 12
HD = 128
SCALE = math.log2(math.e) / math.sqrt(HD)
DEAD = -1e30
COARSE_LANE = 384
COUNT_LANE = 512
META_LANES = 640
EARLY = 7

VMEM = pltpu.VMEM
MEMORY = {"any": jax.ShapeDtypeStruct, "vmem": pltpu.VMEM, "hbm": pltpu.HBM, "scalar": jax.ShapeDtypeStruct}
SPACE = {"scalar": pltpu.SMEM, "hbm": pltpu.HBM}
NT = (((1,), (1,)), ((), ()))


def dot(a, b):
    return jnp.dot(a, b, preferred_element_type=jnp.float32)


def dot_nt(a, b):
    return lax.dot_general(a, b, NT, preferred_element_type=jnp.float32)


def column(row):
    n = row.shape[1]
    shape = (n, n)
    diagonal = lax.broadcasted_iota(jnp.int32, shape, 0) == lax.broadcasted_iota(jnp.int32, shape, 1)
    return jnp.sum(jnp.where(diagonal, jnp.broadcast_to(row, shape), 0.0), axis=1, keepdims=True)


def log_mult(mult):
    return jnp.where(mult > 0.0, jnp.log2(jnp.maximum(mult, 1.0)), DEAD)


def coarse_kernel(
    index_hbm, adjacency_hbm, keys_hbm, values_hbm, coarse_ref, near_ref, keys_ref, values_ref, index_ref, adjacency_ref, sems
):
    load_index = pltpu.make_async_copy(index_hbm, index_ref, sems.at[0])
    load_adjacency = pltpu.make_async_copy(adjacency_hbm, adjacency_ref, sems.at[1])
    load_keys = pltpu.make_async_copy(keys_hbm, keys_ref, sems.at[2])
    load_values = pltpu.make_async_copy(values_hbm, values_ref, sems.at[3])
    for load in (load_index, load_adjacency, load_keys, load_values):
        load.start()
    count = index_ref.shape[1]
    rows = keys_ref.shape[0]
    half = adjacency_ref.shape[2]
    side = 1 - lax.rem(lax.axis_index("band"), 2)
    base = pl.multiple_of(side * half, half)
    load_index.wait()
    picked = column(index_ref[...].astype(jnp.float32))
    slots = lax.broadcasted_iota(jnp.int32, (count, rows), 1).astype(jnp.float32)
    choose = (picked == slots).astype(jnp.bfloat16)
    load_adjacency.wait()
    entries = (adjacency_ref[0, pl.ds(side, 1), :] - base).astype(jnp.float32)
    meta = 2 * (half + count)
    among = index_ref[...] - base
    among = jnp.where((among >= 0) & (among < half), among, -1).astype(jnp.float32)
    among = jnp.concatenate([among, jnp.full((1, half - count), -1.0, jnp.float32)], axis=1)
    first = lax.broadcasted_iota(jnp.int32, (16, half), 0) == 0
    near_ref[meta : meta + 16, 0:half] = jnp.where(first, entries, among).astype(jnp.bfloat16)
    load_keys.wait()
    coarse = dot(choose, keys_ref[...]).astype(jnp.bfloat16)
    coarse_ref[0:count, :] = coarse
    near_ref[2 * half : 2 * half + count, :] = coarse
    near_ref[0:half, :] = keys_ref[pl.ds(base, half), :]
    load_values.wait()
    coarse = dot(choose, values_ref[...]).astype(jnp.bfloat16)
    coarse_ref[count : 2 * count, :] = coarse
    near_ref[2 * half + count : meta, :] = coarse
    near_ref[half : 2 * half, :] = values_ref[pl.ds(base, half), :]


def multiplicity(entries, live):
    width = entries.shape[1]
    shape = (width, width)
    slot = lax.broadcasted_iota(jnp.int32, shape, 0)
    row = lax.broadcasted_iota(jnp.int32, shape, 1).astype(jnp.float32)
    hits = jnp.where((column(entries) == row) & (slot < live), 1.0, 0.0)
    return jnp.sum(hits, axis=0, keepdims=True)


def boundary_kernel(
    apart, index_ref, adjacency_ref, counts_ref, keys_ref, values_ref, far_keys_ref, *far_values_refs
):
    width = adjacency_ref.shape[2]
    slots = far_keys_ref.shape[0]
    count = index_ref.shape[1]
    band = lax.axis_index("band")
    odd = lax.rem(band, 2)
    base = pl.multiple_of(odd * width, width)
    entries = (adjacency_ref[0, pl.ds(odd, 1), :] - base).astype(jnp.float32)
    mult = multiplicity(entries, counts_ref[odd, band])
    coarse = column((index_ref[...] - base).astype(jnp.float32))
    coarse = coarse == lax.broadcasted_iota(jnp.int32, (count, width), 1).astype(jnp.float32)
    coarse = jnp.where(coarse, 1.0 if apart else 0.0, 0.0)
    coarse_mult = dot_nt(jnp.broadcast_to(mult.astype(jnp.bfloat16), (16, width)), coarse.astype(jnp.bfloat16))[0:1, :]
    mult = jnp.where(jnp.sum(coarse, axis=0, keepdims=True) > 0.0, 0.0, mult)
    present = (mult > 0.0).astype(jnp.bfloat16)
    square = (width, width)
    before = lax.broadcasted_iota(jnp.int32, square, 0) < lax.broadcasted_iota(jnp.int32, square, 1)
    order = dot(jnp.broadcast_to(present, (16, width)), before.astype(jnp.bfloat16))[0:1, :]
    place = jnp.where(mult > 0.0, order + 1.0, -1.0)
    wanted = lax.broadcasted_iota(jnp.int32, (slots, width), 0)
    choose = jnp.where(wanted.astype(jnp.float32) == place, 1.0, 0.0).astype(jnp.bfloat16)
    rows = pl.ds(base, width)
    slot_mult = dot_nt(jnp.broadcast_to(mult.astype(jnp.bfloat16), (16, width)), choose)[0:1, :]
    far_keys_ref[...] = dot(choose, keys_ref[rows, :]).astype(jnp.bfloat16)
    distinct = jnp.sum(jnp.where(mult > 0.0, 1.0, 0.0), axis=1, keepdims=True)
    pieces = [slot_mult, coarse_mult, jnp.broadcast_to(distinct, (1, META_LANES - COUNT_LANE))]
    starts = [0, COARSE_LANE, COUNT_LANE, META_LANES]
    padded = [
        jnp.concatenate([x, jnp.zeros((1, end - start - x.shape[1]), jnp.float32)], axis=1)
        if end - start > x.shape[1]
        else x
        for x, start, end in zip(pieces, starts, starts[1:])
    ]
    meta = jnp.concatenate(padded, axis=1)
    first = lax.broadcasted_iota(jnp.int32, (16, META_LANES), 0) == 0
    old = far_keys_ref[0:16, 0:META_LANES].astype(jnp.float32)
    far_keys_ref[0:16, 0:META_LANES] = jnp.where(first, meta, old).astype(jnp.bfloat16)
    start = 0
    for ref in far_values_refs:
        cols = slice(start, start + ref.shape[1])
        ref[...] = dot(choose, values_ref[rows, cols]).astype(jnp.bfloat16)
        start = cols.stop


def head(h):
    return slice(h * HD, (h + 1) * HD)


def blank_rows(count):
    return [jnp.zeros((count, HD), jnp.bfloat16)] if count else []


def across_tiles(slab, columns):
    return jnp.concatenate([slab] * (columns // HD), axis=1)


def with_ones(values):
    return jnp.concatenate([values, jnp.ones_like(values)], axis=1)


def near_kernel(
    exact, half, first, index_ref, counts_ref, queries_ref, keys_ref, values_ref, near_ref, sums_ref, *high_ref
):
    rows, count = keys_ref.shape[0], index_ref.shape[1]
    band = lax.axis_index("band")
    odd = lax.rem(band, 2)
    meta = near_ref[near_ref.shape[0] - 16 :, 0:half].astype(jnp.float32)
    mult = multiplicity(meta[0:1, :], counts_ref[odd, band + 1 - 2 * odd])
    row = lax.broadcasted_iota(jnp.int32, (count, half), 1).astype(jnp.float32)
    among = jnp.where(column(meta[1:2, 0:count]) == row, 1.0, 0.0)
    bias = log_mult(mult + jnp.sum(among, axis=0, keepdims=True))
    own = jnp.where(lax.broadcasted_iota(jnp.int32, (rows, count), 0) == index_ref[...], 1.0, 0.0)
    own = 1.0 + jnp.sum(own, axis=1, keepdims=True)
    own = jnp.broadcast_to(own, (rows, HD)).astype(jnp.bfloat16)
    for h in range(sums_ref.shape[0]):
        cols = head(first + h)
        queries = queries_ref[:, cols]
        scores = [
            dot_nt(queries, keys_ref[:, cols]) * SCALE,
            dot_nt(queries, near_ref[0:half, cols]) * SCALE + bias,
        ]
        if exact:
            high = jnp.maximum(*[jnp.max(x, axis=1, keepdims=True) for x in scores])
            scores = [x - high for x in scores]
            high_ref[0][h] = jnp.broadcast_to(high, high_ref[0].shape[1:])
        weights = jnp.concatenate([jnp.exp2(x).astype(jnp.bfloat16) for x in scores], axis=1)
        values = jnp.concatenate([values_ref[:, cols] * own, own], axis=1)
        values = jnp.concatenate([values, with_ones(near_ref[half : 2 * half, cols])], axis=0)
        sums_ref[h] = dot(weights, values)


def far_kernel(exact, groups, half, count, queries_ref, sent_keys_ref, far_keys_ref, near_ref, *refs):
    sums_refs, (accum_ref, weights_ref, state_ref) = refs[:groups], refs[-3:]
    high_ref = refs[groups] if exact else None
    coarse_refs = refs[groups + exact : -3]
    rows = queries_ref.shape[0]
    slots = far_keys_ref.shape[0]
    padded = weights_ref.shape[2]
    bands = lax.axis_size("band")
    band = lax.axis_index("band")
    edge = (band == 0) | (band == bands - 1)

    def meta_of(ref):
        meta = ref[0:16, 0:META_LANES].astype(jnp.float32)
        first = lax.broadcasted_iota(jnp.int32, meta.shape, 0) == 0
        return jnp.sum(jnp.where(first, meta, 0.0), axis=0, keepdims=True)

    mult = jnp.where(edge, 0.0, meta_of(far_keys_ref))
    most = jnp.max(jnp.maximum(mult, meta_of(sent_keys_ref))[:, COUNT_LANE:])
    overflow = (most > slots - 1.0) & jnp.logical_not(edge)
    few = count // 2
    near = 2 * half + (1 - lax.rem(band, 2)) * few
    near_keys = pl.ds(pl.multiple_of(near, few), few)
    near_values = pl.ds(pl.multiple_of(near + count, few), few)
    coarse = few + len(coarse_refs) * count
    pad = padded - coarse - slots
    bias = [
        jnp.zeros((1, few), jnp.float32),
        jnp.log2(1.0 + mult[:, COARSE_LANE : COARSE_LANE + count]),
        jnp.zeros((1, coarse - few - count), jnp.float32),
        log_mult(mult[:, 0:slots]),
    ]
    bias = jnp.concatenate(bias + ([jnp.full((1, pad), DEAD, jnp.float32)] if pad else []), axis=1)
    no_keys = blank_rows(pad)
    no_values = blank_rows(padded - coarse)
    sizes = jnp.zeros((rows, HD), jnp.float32)
    for h in range(H):
        summed = sums_refs[h * groups // H][h % (H // groups)]
        cols = head(h)
        keys = [near_ref[near_keys, cols]] + [ref[0:count, cols] for ref in coarse_refs]
        keys = jnp.concatenate(keys + [far_keys_ref[:, cols]] + no_keys, axis=0)
        values = [near_ref[near_values, cols]] + [ref[count : 2 * count, cols] for ref in coarse_refs]
        values = jnp.concatenate(values + no_values, axis=0)
        scores = dot_nt(queries_ref[:, cols], keys) * SCALE + bias
        if exact:
            old = high_ref[h]
            high = jnp.maximum(old, jnp.max(scores, axis=1, keepdims=True))
            summed = summed * across_tiles(jnp.exp2(old - high), 2 * HD)
            scores = scores - across_tiles(high, padded)
        weights = jnp.exp2(scores)
        summed = summed + dot(weights.astype(jnp.bfloat16), with_ones(values))
        total = summed[:, HD:]
        inverse = 1.0 / total
        sizes = sizes + (total + inverse)
        accum_ref[:, cols] = summed[:, :HD] * inverse
        weights_ref[h] = (weights * across_tiles(inverse, padded)).astype(jnp.bfloat16)
    safe = jnp.max(sizes) < 2.0**60
    state = jnp.where(overflow, 2.0, jnp.where(safe | exact, 0.0, 1.0))
    state_ref[...] = jnp.broadcast_to(state, state_ref.shape)


def far_share(coarse, h, weights_ref, part, far_values):
    slots, padded = far_values.shape[0], weights_ref.shape[2]
    values = jnp.concatenate(blank_rows(coarse) + [far_values] + blank_rows(padded - coarse - slots), axis=0)
    return dot(weights_ref[h, part, :], values)


def early_kernel(coarse, state_in, accum_ref, weights_ref, far_values_ref, attended_ref, state_ref):
    everything = pl.ds(0, accum_ref.shape[0])
    state_ref[0] = jnp.max(state_in[...]).astype(jnp.int32)
    for h in range(far_values_ref.shape[1] // HD):
        cols = head(h)
        share = far_share(coarse, h, weights_ref, everything, far_values_ref[:, cols])
        attended_ref[:, cols] = accum_ref[:, cols] + share


def project_kernel(coarse, done, accum_ref, weights_ref, far_values_ref, gain_ref, matrix_ref, *refs):
    attended_ref, (out_hbm, normed_ref, out_ref, sems) = refs[0] if done else None, refs[-4:]
    rows, width = accum_ref.shape
    part_rows = rows // 2
    copies = []

    def attended(part, h):
        if h < done:
            return attended_ref[part, head(h)]
        share = far_share(coarse, h, weights_ref, part, far_values_ref[:, head(h - done)])
        return accum_ref[part, head(h)] + share

    def centred(heads):
        center = jnp.sum(functools.reduce(jnp.add, heads), axis=1, keepdims=True) * (1.0 / width)
        heads = [x - center for x in heads]
        square = functools.reduce(jnp.add, [x * x for x in heads])
        spread = jnp.sum(square, axis=1, keepdims=True) * (1.0 / width)
        return heads, lax.rsqrt(spread + 1e-05)

    def norm(part, heads, inverse):
        for h, x in enumerate(heads):
            normed_ref[part, head(h)] = (x * inverse * gain_ref[:, head(h)]).astype(jnp.bfloat16)

    def project(part, start, stop):
        cols = slice(start * width // 6, stop * width // 6)
        out_ref[part, cols] = dot(normed_ref[part, :], matrix_ref[:, cols]).astype(jnp.bfloat16)

    def send(part, start, stop):
        block = (part, pl.ds(start * width // 6, (stop - start) * width // 6))
        copies.append(pltpu.make_async_copy(out_ref.at[block], out_hbm.at[block], sems.at[len(copies)]))
        copies[-1].start()

    one, two = pl.ds(0, part_rows), pl.ds(part_rows, part_rows)
    norm(one, *centred([attended(one, h) for h in range(H)]))
    heads = []
    for i in range(3):
        heads += [attended(two, h) for h in range(4 * i, 4 * i + 4)]
        project(one, i, i + 1)
    heads, inverse = centred(heads)
    project(one, 3, 4)
    norm(two, heads, inverse)
    project(one, 4, 6)
    send(one, 0, 6)
    for i in range(0, 6, 2):
        project(two, i, i + 2)
        send(two, i, i + 2)
    for copy in copies:
        copy.wait()


def spec(space=VMEM):
    return pl.BlockSpec(memory_space=space)


def call(kernel, ins, outs, scratch=(), limit=24, cost=None):
    flops, nbytes, exps = cost
    ins = [(pltpu.with_memory_space_constraint(x, s) if s is pltpu.HBM else x, s) for x, s in ins]
    return pl.pallas_call(
        kernel,
        in_specs=[spec(s) for _, s in ins],
        out_specs=tuple(spec(SPACE.get(keep, VMEM)) for _, _, keep in outs),
        out_shape=tuple(
            MEMORY[keep](shape, dtype) for shape, dtype, keep in outs
        ),
        scratch_shapes=list(scratch),
        compiler_params=pltpu.CompilerParams(vmem_limit_bytes=limit << 20),
        cost_estimate=pl.CostEstimate(flops=flops, bytes_accessed=nbytes, transcendentals=exps),
    )(*[x for x, _ in ins])


def on_device(queries, keys, values, out_gain, out_weight, adjacency, send_counts, coarse_index):
    rows, width = queries.shape
    bands = lax.axis_size("band")
    half = adjacency.shape[2]
    count = coarse_index.shape[0]
    slots = (half * 21 // 32 if bands == 4 else half * 11 // 16) // 8 * 8
    bf16, f32 = jnp.bfloat16, jnp.float32
    smem = pltpu.SMEM

    def swap(block, mask):
        return lax.ppermute(block, "band", [(i, i ^ mask) for i in range(bands)])

    def far(block):
        slides = lax.axis_size("slide")
        pairs = []
        for slide in range(slides):
            for band in range(bands):
                end = band in (0, bands - 1)
                to = (slide ^ 1, band) if end else (slide, band + 1 if band % 2 else band - 1)
                pairs.append((slide * bands + band, to[0] * bands + to[1]))
        return lax.ppermute(block, ("slide", "band"), pairs)

    def across(block):
        up = [(i, i + 1) for i in range(1, bands - 1, 2)]
        return lax.ppermute(block, "band", up + [(j, i) for i, j in up])

    early = width * EARLY // H
    index = coarse_index.reshape(1, count)
    others = (bands - 2) * count + count // 2
    after = lambda first, x: lax.optimization_barrier((first, x))[1]
    resident = ((rows, width), bf16, "vmem")
    coarse, near, keys, values = call(
        coarse_kernel,
        [(x, pltpu.HBM) for x in (index, adjacency, keys, values)],
        [((2 * count, width), bf16, "any"), ((2 * (half + count) + 16, width), bf16, "any"), resident, resident],
        scratch=[
            pltpu.VMEM((1, count), jnp.int32),
            pltpu.VMEM(adjacency.shape, jnp.int32),
            pltpu.SemaphoreType.DMA((4,)),
        ],
        cost=(4 * count * rows * width, 4 * rows * width, 0),
    )
    mirrored = swap(coarse, bands - 1)
    near = swap(near, 1)
    send_counts = send_counts.T

    def boundary(slots):
        return call(
            functools.partial(boundary_kernel, bands == 4),
            [(index, VMEM), (adjacency, VMEM), (send_counts, smem), (keys, VMEM), (values, VMEM)],
            [((slots, columns), bf16, "any") for columns in (width, early, width - early)],
            cost=(1, 1, 0),
        )

    def near_sums(exact, keys, first, heads):
        wide = ((heads, rows, 2 * HD), f32, "vmem")
        return call(
            functools.partial(near_kernel, exact, half, first),
            [(index, VMEM), (send_counts, smem)] + [(x, VMEM) for x in [queries, keys, values, near]],
            [wide, ((heads, rows, HD), f32, "vmem")] if exact else [wide],
            cost=((21 if first else 0) * rows * half * width, 2, 0),
        )

    def far_weights(exact, states, sent_keys, far_keys):
        slots = far_keys.shape[0]
        padded = -(-(others + slots) // HD) * HD
        return call(
            functools.partial(far_kernel, exact, len(states) - exact, half, count),
            [(x, VMEM) for x in [queries, sent_keys, far_keys, near] + list(states) + pieces[1:]],
            [((rows, width), f32, "vmem"), ((H, rows, padded), bf16, "vmem"), ((8, HD), f32, "vmem")],
            cost=(4 * rows * slots * width, 2 * rows * width, H * rows * slots),
        )

    def project(done, accum, weights, far_values, *attended):
        operands = (accum, weights, far_values, gain, out_weight, *attended)
        return call(
            functools.partial(project_kernel, others, done),
            [(x, VMEM) for x in operands],
            [((rows, width), bf16, "hbm")],
            scratch=[
                pltpu.VMEM((rows, width), bf16),
                pltpu.VMEM((rows, width), bf16),
                pltpu.SemaphoreType.DMA((4,)),
            ],
            cost=(2 * rows * width * (half + width), 2 * width * width, 0),
        )[0]

    sent_keys, *sent_values = boundary(slots)
    far_keys = far(sent_keys)
    far_values = [far(sent_values[0])]
    own_keys = after(sent_keys, keys)
    half_heads = H // 2
    (first,) = near_sums(False, own_keys, 0, half_heads)
    mirrored = after(first, mirrored)
    (second,) = near_sums(False, after(mirrored, own_keys), half_heads, H - half_heads)
    states = [first, second]
    far_values.append(far(after(second, sent_values[1])))
    pieces = [coarse, mirrored, swap(mirrored, 1)]
    near_piece = near[2 * half : 2 * (half + count)] if bands > 4 else None
    for mask in [1 << i for i in range(1, bands.bit_length() - 2)]:
        pieces = pieces + [swap(piece, mask) for piece in pieces + [near_piece]]
    accum, weights, state = far_weights(False, states, sent_keys, far_keys)
    gain = after(accum, out_gain.reshape(1, width))
    attended, state = call(
        functools.partial(early_kernel, others),
        [(x, VMEM) for x in [state, accum, weights, far_values[0]]],
        [((rows, early), f32, "vmem"), ((1,), jnp.int32, "scalar")],
        cost=(16 * rows * slots * width, 2 * rows * early, 0),
    )

    def fine():
        return project(early // HD, accum, weights, far_values[1], attended)

    def exact():
        accum, weights, _ = far_weights(True, near_sums(True, keys, 0, H), sent_keys, far_keys)
        return project(0, accum, weights, jnp.concatenate(far_values, axis=1))

    def all_rows():
        sent_keys, *sent_values = boundary(half + 16)
        far_keys, far_values = across(sent_keys), across(jnp.concatenate(sent_values, axis=1))
        accum, weights, _ = far_weights(True, near_sums(True, keys, 0, H), sent_keys, far_keys)
        return project(0, accum, weights, far_values)

    return lax.switch(state[0], [fine, exact, all_rows])


def solution(mesh):
    in_specs = (
        P(("slide", "band"), None),
        P(("slide", "band"), None),
        P(("slide", "band"), None),
        P(),
        P(),
        P(("slide", "band"), None, None),
        P("slide", None),
        P(("slide", "band")),
    )
    out_specs = P(("slide", "band"), None)
    return jax.shard_map(
        on_device, mesh=mesh, in_specs=in_specs, out_specs=out_specs, check_vma=False
    )
```

```python
import functools
import math

import jax
import jax.numpy as jnp
from jax import lax
from jax.experimental import pallas as pl
from jax.experimental.pallas import tpu as pltpu
from jax.sharding import PartitionSpec as P

H = 12
HD = 128
SCALE = math.log2(math.e) / math.sqrt(HD)
DEAD = -1e30
COARSE_LANE = 384
COUNT_LANE = 512
META_LANES = 640
EARLY = 7

VMEM = pltpu.VMEM
MEMORY = {"any": jax.ShapeDtypeStruct, "vmem": pltpu.VMEM, "hbm": pltpu.HBM, "scalar": jax.ShapeDtypeStruct}
SPACE = {"scalar": pltpu.SMEM, "hbm": pltpu.HBM}
NT = (((1,), (1,)), ((), ()))


def dot(a, b):
    return jnp.dot(a, b, preferred_element_type=jnp.float32)


def dot_nt(a, b):
    return lax.dot_general(a, b, NT, preferred_element_type=jnp.float32)


def column(row):
    n = row.shape[1]
    shape = (n, n)
    diagonal = lax.broadcasted_iota(jnp.int32, shape, 0) == lax.broadcasted_iota(jnp.int32, shape, 1)
    return jnp.sum(jnp.where(diagonal, jnp.broadcast_to(row, shape), 0.0), axis=1, keepdims=True)


def log_mult(mult):
    return jnp.where(mult > 0.0, jnp.log2(jnp.maximum(mult, 1.0)), DEAD)


def coarse_kernel(
    index_hbm, adjacency_hbm, keys_hbm, values_hbm, coarse_ref, near_ref, keys_ref, values_ref, index_ref, adjacency_ref, sems
):
    count = index_ref.shape[1]
    rows = keys_ref.shape[0]
    half = adjacency_ref.shape[2]
    few = count // 2
    load_index = pltpu.make_async_copy(index_hbm, index_ref, sems.at[0])
    load_adjacency = pltpu.make_async_copy(adjacency_hbm, adjacency_ref, sems.at[1])
    loads = []
    for source, to in ((keys_hbm, keys_ref), (values_hbm, values_ref)):
        for start in (0, half):
            part = pl.ds(start, half)
            loads.append(pltpu.make_async_copy(source.at[part], to.at[part], sems.at[2 + len(loads)]))
    for load in (load_index, load_adjacency, *loads):
        load.start()
    side = 1 - lax.rem(lax.axis_index("band"), 2)
    base = pl.multiple_of(side * half, half)
    load_index.wait()
    picked = column(index_ref[...].astype(jnp.float32))
    slots = lax.broadcasted_iota(jnp.int32, (count, rows), 1).astype(jnp.float32)
    choose = (picked == slots).astype(jnp.bfloat16)
    load_adjacency.wait()
    entries = (adjacency_ref[0, pl.ds(side, 1), :] - base).astype(jnp.float32)
    meta = 2 * (half + count)
    among = index_ref[...] - base
    among = jnp.where((among >= 0) & (among < half), among, -1).astype(jnp.float32)
    among = jnp.concatenate([among, jnp.full((1, half - count), -1.0, jnp.float32)], axis=1)
    first = lax.broadcasted_iota(jnp.int32, (16, half), 0) == 0
    near_ref[meta : meta + 16, 0:half] = jnp.where(first, entries, among).astype(jnp.bfloat16)
    for i, load in enumerate(loads):
        load.wait()
        ref = (keys_ref, values_ref)[i // 2]
        mine, theirs = (i % 2) * few, (i % 2) * half
        coarse = dot(choose[mine : mine + few, theirs : theirs + half], ref[theirs : theirs + half, :]).astype(jnp.bfloat16)
        to = i // 2 * count + mine
        coarse_ref[to : to + few, :] = coarse
        near_ref[2 * half + to : 2 * half + to + few, :] = coarse
        if i % 2:
            near_ref[i // 2 * half : i // 2 * half + half, :] = ref[pl.ds(base, half), :]


def multiplicity(entries, live):
    width = entries.shape[1]
    shape = (width, width)
    slot = lax.broadcasted_iota(jnp.int32, shape, 0)
    row = lax.broadcasted_iota(jnp.int32, shape, 1).astype(jnp.float32)
    hits = jnp.where((column(entries) == row) & (slot < live), 1.0, 0.0)
    return jnp.sum(hits, axis=0, keepdims=True)


def boundary_kernel(
    apart, index_ref, adjacency_ref, counts_ref, keys_ref, values_ref, far_keys_ref, *far_values_refs
):
    width = adjacency_ref.shape[2]
    slots = far_keys_ref.shape[0]
    count = index_ref.shape[1]
    band = lax.axis_index("band")
    odd = lax.rem(band, 2)
    base = pl.multiple_of(odd * width, width)
    entries = (adjacency_ref[0, pl.ds(odd, 1), :] - base).astype(jnp.float32)
    mult = multiplicity(entries, counts_ref[odd, band])
    coarse = column((index_ref[...] - base).astype(jnp.float32))
    coarse = coarse == lax.broadcasted_iota(jnp.int32, (count, width), 1).astype(jnp.float32)
    coarse = jnp.where(coarse, 1.0 if apart else 0.0, 0.0)
    coarse_mult = dot_nt(jnp.broadcast_to(mult.astype(jnp.bfloat16), (16, width)), coarse.astype(jnp.bfloat16))[0:1, :]
    mult = jnp.where(jnp.sum(coarse, axis=0, keepdims=True) > 0.0, 0.0, mult)
    present = (mult > 0.0).astype(jnp.bfloat16)
    square = (width, width)
    before = lax.broadcasted_iota(jnp.int32, square, 0) < lax.broadcasted_iota(jnp.int32, square, 1)
    order = dot(jnp.broadcast_to(present, (16, width)), before.astype(jnp.bfloat16))[0:1, :]
    place = jnp.where(mult > 0.0, order + 1.0, -1.0)
    wanted = lax.broadcasted_iota(jnp.int32, (slots, width), 0)
    choose = jnp.where(wanted.astype(jnp.float32) == place, 1.0, 0.0).astype(jnp.bfloat16)
    rows = pl.ds(base, width)
    slot_mult = dot_nt(jnp.broadcast_to(mult.astype(jnp.bfloat16), (16, width)), choose)[0:1, :]
    far_keys_ref[...] = dot(choose, keys_ref[rows, :]).astype(jnp.bfloat16)
    distinct = jnp.sum(jnp.where(mult > 0.0, 1.0, 0.0), axis=1, keepdims=True)
    pieces = [slot_mult, coarse_mult, jnp.broadcast_to(distinct, (1, META_LANES - COUNT_LANE))]
    starts = [0, COARSE_LANE, COUNT_LANE, META_LANES]
    padded = [
        jnp.concatenate([x, jnp.zeros((1, end - start - x.shape[1]), jnp.float32)], axis=1)
        if end - start > x.shape[1]
        else x
        for x, start, end in zip(pieces, starts, starts[1:])
    ]
    meta = jnp.concatenate(padded, axis=1)
    first = lax.broadcasted_iota(jnp.int32, (16, META_LANES), 0) == 0
    old = far_keys_ref[0:16, 0:META_LANES].astype(jnp.float32)
    far_keys_ref[0:16, 0:META_LANES] = jnp.where(first, meta, old).astype(jnp.bfloat16)
    start = 0
    for ref in far_values_refs:
        cols = slice(start, start + ref.shape[1])
        ref[...] = dot(choose, values_ref[rows, cols]).astype(jnp.bfloat16)
        start = cols.stop


def head(h):
    return slice(h * HD, (h + 1) * HD)


def blank_rows(count):
    return [jnp.zeros((count, HD), jnp.bfloat16)] if count else []


def across_tiles(slab, columns):
    return jnp.concatenate([slab] * (columns // HD), axis=1)


def with_ones(values):
    return jnp.concatenate([values, jnp.ones_like(values)], axis=1)


def near_kernel(
    exact, half, first, index_ref, counts_ref, queries_ref, keys_ref, values_ref, near_ref, sums_ref, *high_ref
):
    rows, count = keys_ref.shape[0], index_ref.shape[1]
    band = lax.axis_index("band")
    odd = lax.rem(band, 2)
    meta = near_ref[near_ref.shape[0] - 16 :, 0:half].astype(jnp.float32)
    mult = multiplicity(meta[0:1, :], counts_ref[odd, band + 1 - 2 * odd])
    row = lax.broadcasted_iota(jnp.int32, (count, half), 1).astype(jnp.float32)
    among = jnp.where(column(meta[1:2, 0:count]) == row, 1.0, 0.0)
    bias = log_mult(mult + jnp.sum(among, axis=0, keepdims=True))
    own = jnp.where(lax.broadcasted_iota(jnp.int32, (rows, count), 0) == index_ref[...], 1.0, 0.0)
    own = 1.0 + jnp.sum(own, axis=1, keepdims=True)
    own = jnp.broadcast_to(own, (rows, HD)).astype(jnp.bfloat16)
    for h in range(sums_ref.shape[0]):
        cols = head(first + h)
        queries = queries_ref[:, cols]
        scores = [
            dot_nt(queries, keys_ref[:, cols]) * SCALE,
            dot_nt(queries, near_ref[0:half, cols]) * SCALE + bias,
        ]
        if exact:
            high = jnp.maximum(*[jnp.max(x, axis=1, keepdims=True) for x in scores])
            scores = [x - high for x in scores]
            high_ref[0][h] = jnp.broadcast_to(high, high_ref[0].shape[1:])
        weights = jnp.concatenate([jnp.exp2(x).astype(jnp.bfloat16) for x in scores], axis=1)
        values = jnp.concatenate([values_ref[:, cols] * own, own], axis=1)
        values = jnp.concatenate([values, with_ones(near_ref[half : 2 * half, cols])], axis=0)
        sums_ref[h] = dot(weights, values)


def far_kernel(exact, groups, half, count, queries_ref, sent_keys_ref, far_keys_ref, near_ref, *refs):
    sums_refs, (accum_ref, weights_ref, state_ref) = refs[:groups], refs[-3:]
    high_ref = refs[groups] if exact else None
    coarse_refs = refs[groups + exact : -3]
    rows = queries_ref.shape[0]
    slots = far_keys_ref.shape[0]
    padded = weights_ref.shape[2]
    bands = lax.axis_size("band")
    band = lax.axis_index("band")
    edge = (band == 0) | (band == bands - 1)

    def meta_of(ref):
        meta = ref[0:16, 0:META_LANES].astype(jnp.float32)
        first = lax.broadcasted_iota(jnp.int32, meta.shape, 0) == 0
        return jnp.sum(jnp.where(first, meta, 0.0), axis=0, keepdims=True)

    mult = jnp.where(edge, 0.0, meta_of(far_keys_ref))
    most = jnp.max(jnp.maximum(mult, meta_of(sent_keys_ref))[:, COUNT_LANE:])
    overflow = (most > slots - 1.0) & jnp.logical_not(edge)
    few = count // 2
    near = 2 * half + (1 - lax.rem(band, 2)) * few
    near_keys = pl.ds(pl.multiple_of(near, few), few)
    near_values = pl.ds(pl.multiple_of(near + count, few), few)
    coarse = few + len(coarse_refs) * count
    pad = padded - coarse - slots
    bias = [
        jnp.zeros((1, few), jnp.float32),
        jnp.log2(1.0 + mult[:, COARSE_LANE : COARSE_LANE + count]),
        jnp.zeros((1, coarse - few - count), jnp.float32),
        log_mult(mult[:, 0:slots]),
    ]
    bias = jnp.concatenate(bias + ([jnp.full((1, pad), DEAD, jnp.float32)] if pad else []), axis=1)
    no_keys = blank_rows(pad)
    no_values = blank_rows(padded - coarse)
    sizes = jnp.zeros((rows, HD), jnp.float32)
    for h in range(H):
        summed = sums_refs[h * groups // H][h % (H // groups)]
        cols = head(h)
        keys = [near_ref[near_keys, cols]] + [ref[0:count, cols] for ref in coarse_refs]
        keys = jnp.concatenate(keys + [far_keys_ref[:, cols]] + no_keys, axis=0)
        values = [near_ref[near_values, cols]] + [ref[count : 2 * count, cols] for ref in coarse_refs]
        values = jnp.concatenate(values + no_values, axis=0)
        scores = dot_nt(queries_ref[:, cols], keys) * SCALE + bias
        if exact:
            old = high_ref[h]
            high = jnp.maximum(old, jnp.max(scores, axis=1, keepdims=True))
            summed = summed * across_tiles(jnp.exp2(old - high), 2 * HD)
            scores = scores - across_tiles(high, padded)
        weights = jnp.exp2(scores)
        summed = summed + dot(weights.astype(jnp.bfloat16), with_ones(values))
        total = summed[:, HD:]
        inverse = 1.0 / total
        sizes = sizes + (total + inverse)
        accum_ref[:, cols] = summed[:, :HD] * inverse
        weights_ref[h] = (weights * across_tiles(inverse, padded)).astype(jnp.bfloat16)
    safe = jnp.max(sizes) < 2.0**60
    state = jnp.where(overflow, 2.0, jnp.where(safe | exact, 0.0, 1.0))
    state_ref[...] = jnp.broadcast_to(state, state_ref.shape)


def far_share(coarse, h, weights_ref, part, far_values):
    slots, padded = far_values.shape[0], weights_ref.shape[2]
    values = jnp.concatenate(blank_rows(coarse) + [far_values] + blank_rows(padded - coarse - slots), axis=0)
    return dot(weights_ref[h, part, :], values)


def early_kernel(coarse, state_in, accum_ref, weights_ref, far_values_ref, attended_ref, state_ref):
    everything = pl.ds(0, accum_ref.shape[0])
    state_ref[0] = jnp.max(state_in[...]).astype(jnp.int32)
    for h in range(far_values_ref.shape[1] // HD):
        cols = head(h)
        share = far_share(coarse, h, weights_ref, everything, far_values_ref[:, cols])
        attended_ref[:, cols] = accum_ref[:, cols] + share


def project_kernel(coarse, done, accum_ref, weights_ref, far_values_ref, gain_ref, matrix_ref, *refs):
    attended_ref, (out_hbm, normed_ref, out_ref, sems) = refs[0] if done else None, refs[-4:]
    rows, width = accum_ref.shape
    part_rows = rows // 2
    copies = []

    def attended(part, h):
        if h < done:
            return attended_ref[part, head(h)]
        share = far_share(coarse, h, weights_ref, part, far_values_ref[:, head(h - done)])
        return accum_ref[part, head(h)] + share

    def centred(heads):
        center = jnp.sum(functools.reduce(jnp.add, heads), axis=1, keepdims=True) * (1.0 / width)
        heads = [x - center for x in heads]
        square = functools.reduce(jnp.add, [x * x for x in heads])
        spread = jnp.sum(square, axis=1, keepdims=True) * (1.0 / width)
        return heads, lax.rsqrt(spread + 1e-05)

    def norm(part, heads, inverse):
        for h, x in enumerate(heads):
            normed_ref[part, head(h)] = (x * inverse * gain_ref[:, head(h)]).astype(jnp.bfloat16)

    def project(part, start, stop):
        cols = slice(start * width // 6, stop * width // 6)
        out_ref[part, cols] = dot(normed_ref[part, :], matrix_ref[:, cols]).astype(jnp.bfloat16)

    def send(part, start, stop):
        block = (part, pl.ds(start * width // 6, (stop - start) * width // 6))
        copies.append(pltpu.make_async_copy(out_ref.at[block], out_hbm.at[block], sems.at[len(copies)]))
        copies[-1].start()

    one, two = pl.ds(0, part_rows), pl.ds(part_rows, part_rows)
    norm(one, *centred([attended(one, h) for h in range(H)]))
    heads = []
    for i in range(3):
        heads += [attended(two, h) for h in range(4 * i, 4 * i + 4)]
        project(one, i, i + 1)
    heads, inverse = centred(heads)
    project(one, 3, 4)
    norm(two, heads, inverse)
    project(one, 4, 6)
    send(one, 0, 6)
    for i in range(0, 6, 2):
        project(two, i, i + 2)
        send(two, i, i + 2)
    for copy in copies:
        copy.wait()


def spec(space=VMEM):
    return pl.BlockSpec(memory_space=space)


def call(kernel, ins, outs, scratch=(), limit=24, cost=None):
    flops, nbytes, exps = cost
    ins = [(pltpu.with_memory_space_constraint(x, s) if s is pltpu.HBM else x, s) for x, s in ins]
    return pl.pallas_call(
        kernel,
        in_specs=[spec(s) for _, s in ins],
        out_specs=tuple(spec(SPACE.get(keep, VMEM)) for _, _, keep in outs),
        out_shape=tuple(
            MEMORY[keep](shape, dtype) for shape, dtype, keep in outs
        ),
        scratch_shapes=list(scratch),
        compiler_params=pltpu.CompilerParams(vmem_limit_bytes=limit << 20),
        cost_estimate=pl.CostEstimate(flops=flops, bytes_accessed=nbytes, transcendentals=exps),
    )(*[x for x, _ in ins])


def on_device(queries, keys, values, out_gain, out_weight, adjacency, send_counts, coarse_index):
    rows, width = queries.shape
    bands = lax.axis_size("band")
    half = adjacency.shape[2]
    count = coarse_index.shape[0]
    slots = (half * 21 // 32 if bands == 4 else half * 11 // 16) // 8 * 8
    bf16, f32 = jnp.bfloat16, jnp.float32
    smem = pltpu.SMEM

    def swap(block, mask):
        return lax.ppermute(block, "band", [(i, i ^ mask) for i in range(bands)])

    def far(block):
        slides = lax.axis_size("slide")
        pairs = []
        for slide in range(slides):
            for band in range(bands):
                end = band in (0, bands - 1)
                to = (slide ^ 1, band) if end else (slide, band + 1 if band % 2 else band - 1)
                pairs.append((slide * bands + band, to[0] * bands + to[1]))
        return lax.ppermute(block, ("slide", "band"), pairs)

    def across(block):
        up = [(i, i + 1) for i in range(1, bands - 1, 2)]
        return lax.ppermute(block, "band", up + [(j, i) for i, j in up])

    early = width * EARLY // H
    index = coarse_index.reshape(1, count)
    others = (bands - 2) * count + count // 2
    after = lambda first, x: lax.optimization_barrier((first, x))[1]
    resident = ((rows, width), bf16, "vmem")
    coarse, near, keys, values = call(
        coarse_kernel,
        [(x, pltpu.HBM) for x in (index, adjacency, keys, values)],
        [((2 * count, width), bf16, "any"), ((2 * (half + count) + 16, width), bf16, "any"), resident, resident],
        scratch=[
            pltpu.VMEM((1, count), jnp.int32),
            pltpu.VMEM(adjacency.shape, jnp.int32),
            pltpu.SemaphoreType.DMA((6,)),
        ],
        cost=(4 * count * rows * width, 4 * rows * width, 0),
    )
    mirrored = swap(coarse, bands - 1)
    near = swap(near, 1)
    send_counts = send_counts.T

    def boundary(slots):
        return call(
            functools.partial(boundary_kernel, bands == 4),
            [(index, VMEM), (adjacency, VMEM), (send_counts, smem), (keys, VMEM), (values, VMEM)],
            [((slots, columns), bf16, "any") for columns in (width, early, width - early)],
            cost=(1, 1, 0),
        )

    def near_sums(exact, keys, first, heads):
        wide = ((heads, rows, 2 * HD), f32, "vmem")
        return call(
            functools.partial(near_kernel, exact, half, first),
            [(index, VMEM), (send_counts, smem)] + [(x, VMEM) for x in [queries, keys, values, near]],
            [wide, ((heads, rows, HD), f32, "vmem")] if exact else [wide],
            cost=((21 if first else 0) * rows * half * width, 2, 0),
        )

    def far_weights(exact, states, sent_keys, far_keys):
        slots = far_keys.shape[0]
        padded = -(-(others + slots) // HD) * HD
        return call(
            functools.partial(far_kernel, exact, len(states) - exact, half, count),
            [(x, VMEM) for x in [queries, sent_keys, far_keys, near] + list(states) + pieces[1:]],
            [((rows, width), f32, "vmem"), ((H, rows, padded), bf16, "vmem"), ((8, HD), f32, "vmem")],
            cost=(4 * rows * slots * width, 2 * rows * width, H * rows * slots),
        )

    def project(done, accum, weights, far_values, *attended):
        operands = (accum, weights, far_values, gain, out_weight, *attended)
        return call(
            functools.partial(project_kernel, others, done),
            [(x, VMEM) for x in operands],
            [((rows, width), bf16, "hbm")],
            scratch=[
                pltpu.VMEM((rows, width), bf16),
                pltpu.VMEM((rows, width), bf16),
                pltpu.SemaphoreType.DMA((4,)),
            ],
            cost=(2 * rows * width * (half + width), 2 * width * width, 0),
        )[0]

    sent_keys, *sent_values = boundary(slots)
    far_keys = far(sent_keys)
    far_values = [far(sent_values[0])]
    own_keys = after(sent_keys, keys)
    half_heads = H // 2
    (first,) = near_sums(False, own_keys, 0, half_heads)
    mirrored = after(first, mirrored)
    (second,) = near_sums(False, after(mirrored, own_keys), half_heads, H - half_heads)
    states = [first, second]
    far_values.append(far(after(second, sent_values[1])))
    pieces = [coarse, mirrored, swap(mirrored, 1)]
    near_piece = near[2 * half : 2 * (half + count)] if bands > 4 else None
    for mask in [1 << i for i in range(1, bands.bit_length() - 2)]:
        pieces = pieces + [swap(piece, mask) for piece in pieces + [near_piece]]
    accum, weights, state = far_weights(False, states, sent_keys, far_keys)
    gain = after(accum, out_gain.reshape(1, width))
    attended, state = call(
        functools.partial(early_kernel, others),
        [(x, VMEM) for x in [state, accum, weights, far_values[0]]],
        [((rows, early), f32, "vmem"), ((1,), jnp.int32, "scalar")],
        cost=(16 * rows * slots * width, 2 * rows * early, 0),
    )

    def fine():
        return project(early // HD, accum, weights, far_values[1], attended)

    def exact():
        accum, weights, _ = far_weights(True, near_sums(True, keys, 0, H), sent_keys, far_keys)
        return project(0, accum, weights, jnp.concatenate(far_values, axis=1))

    def all_rows():
        sent_keys, *sent_values = boundary(half + 16)
        far_keys, far_values = across(sent_keys), across(jnp.concatenate(sent_values, axis=1))
        accum, weights, _ = far_weights(True, near_sums(True, keys, 0, H), sent_keys, far_keys)
        return project(0, accum, weights, far_values)

    return lax.switch(state[0], [fine, exact, all_rows])


def solution(mesh):
    in_specs = (
        P(("slide", "band"), None),
        P(("slide", "band"), None),
        P(("slide", "band"), None),
        P(),
        P(),
        P(("slide", "band"), None, None),
        P("slide", None),
        P(("slide", "band")),
    )
    out_specs = P(("slide", "band"), None)
    return jax.shard_map(
        on_device, mesh=mesh, in_specs=in_specs, out_specs=out_specs, check_vma=False
    )
```

```python
import functools
import math

import jax
import jax.numpy as jnp
from jax import lax
from jax.experimental import pallas as pl
from jax.experimental.pallas import tpu as pltpu
from jax.sharding import PartitionSpec as P

H = 12
HD = 128
SCALE = math.log2(math.e) / math.sqrt(HD)
DEAD = -1e30
COARSE_LANE = 384
COUNT_LANE = 512
META_LANES = 640
EARLY = 8

VMEM = pltpu.VMEM
MEMORY = {"any": jax.ShapeDtypeStruct, "vmem": pltpu.VMEM, "hbm": pltpu.HBM, "scalar": jax.ShapeDtypeStruct}
SPACE = {"scalar": pltpu.SMEM, "hbm": pltpu.HBM}
NT = (((1,), (1,)), ((), ()))


def dot(a, b):
    return jnp.dot(a, b, preferred_element_type=jnp.float32)


def dot_nt(a, b):
    return lax.dot_general(a, b, NT, preferred_element_type=jnp.float32)


def column(row):
    n = row.shape[1]
    shape = (n, n)
    diagonal = lax.broadcasted_iota(jnp.int32, shape, 0) == lax.broadcasted_iota(jnp.int32, shape, 1)
    return jnp.sum(jnp.where(diagonal, jnp.broadcast_to(row, shape), 0.0), axis=1, keepdims=True)


def log_mult(mult):
    return jnp.where(mult > 0.0, jnp.log2(jnp.maximum(mult, 1.0)), DEAD)


def coarse_kernel(
    index_hbm, adjacency_hbm, keys_hbm, values_hbm, coarse_ref, near_ref, keys_ref, values_ref, index_ref, adjacency_ref, sems
):
    count = index_ref.shape[1]
    rows = keys_ref.shape[0]
    half = adjacency_ref.shape[2]
    few = count // 2
    load_index = pltpu.make_async_copy(index_hbm, index_ref, sems.at[0])
    load_adjacency = pltpu.make_async_copy(adjacency_hbm, adjacency_ref, sems.at[1])
    loads = []
    for source, to in ((keys_hbm, keys_ref), (values_hbm, values_ref)):
        for start in (0, half):
            part = pl.ds(start, half)
            loads.append(pltpu.make_async_copy(source.at[part], to.at[part], sems.at[2 + len(loads)]))
    for load in (load_index, load_adjacency, *loads):
        load.start()
    side = 1 - lax.rem(lax.axis_index("band"), 2)
    base = pl.multiple_of(side * half, half)
    load_index.wait()
    picked = column(index_ref[...].astype(jnp.float32))
    slots = lax.broadcasted_iota(jnp.int32, (count, rows), 1).astype(jnp.float32)
    choose = (picked == slots).astype(jnp.bfloat16)
    load_adjacency.wait()
    entries = (adjacency_ref[0, pl.ds(side, 1), :] - base).astype(jnp.float32)
    meta = 2 * (half + count)
    among = index_ref[...] - base
    among = jnp.where((among >= 0) & (among < half), among, -1).astype(jnp.float32)
    among = jnp.concatenate([among, jnp.full((1, half - count), -1.0, jnp.float32)], axis=1)
    first = lax.broadcasted_iota(jnp.int32, (16, half), 0) == 0
    near_ref[meta : meta + 16, 0:half] = jnp.where(first, entries, among).astype(jnp.bfloat16)
    for i, load in enumerate(loads):
        load.wait()
        ref = (keys_ref, values_ref)[i // 2]
        mine, theirs = (i % 2) * few, (i % 2) * half
        coarse = dot(choose[mine : mine + few, theirs : theirs + half], ref[theirs : theirs + half, :]).astype(jnp.bfloat16)
        to = i // 2 * count + mine
        coarse_ref[to : to + few, :] = coarse
        near_ref[2 * half + to : 2 * half + to + few, :] = coarse
        if i % 2:
            near_ref[i // 2 * half : i // 2 * half + half, :] = ref[pl.ds(base, half), :]


def multiplicity(entries, live):
    width = entries.shape[1]
    shape = (width, width)
    slot = lax.broadcasted_iota(jnp.int32, shape, 0)
    row = lax.broadcasted_iota(jnp.int32, shape, 1).astype(jnp.float32)
    hits = jnp.where((column(entries) == row) & (slot < live), 1.0, 0.0)
    return jnp.sum(hits, axis=0, keepdims=True)


def boundary_kernel(
    apart, index_ref, adjacency_ref, counts_ref, keys_ref, values_ref, far_keys_ref, *far_values_refs
):
    width = adjacency_ref.shape[2]
    slots = far_keys_ref.shape[0]
    count = index_ref.shape[1]
    band = lax.axis_index("band")
    odd = lax.rem(band, 2)
    base = pl.multiple_of(odd * width, width)
    entries = (adjacency_ref[0, pl.ds(odd, 1), :] - base).astype(jnp.float32)
    mult = multiplicity(entries, counts_ref[odd, band])
    coarse = column((index_ref[...] - base).astype(jnp.float32))
    coarse = coarse == lax.broadcasted_iota(jnp.int32, (count, width), 1).astype(jnp.float32)
    coarse = jnp.where(coarse, 1.0 if apart else 0.0, 0.0)
    coarse_mult = dot_nt(jnp.broadcast_to(mult.astype(jnp.bfloat16), (16, width)), coarse.astype(jnp.bfloat16))[0:1, :]
    mult = jnp.where(jnp.sum(coarse, axis=0, keepdims=True) > 0.0, 0.0, mult)
    present = (mult > 0.0).astype(jnp.bfloat16)
    square = (width, width)
    before = lax.broadcasted_iota(jnp.int32, square, 0) < lax.broadcasted_iota(jnp.int32, square, 1)
    order = dot(jnp.broadcast_to(present, (16, width)), before.astype(jnp.bfloat16))[0:1, :]
    place = jnp.where(mult > 0.0, order + 1.0, -1.0)
    wanted = lax.broadcasted_iota(jnp.int32, (slots, width), 0)
    choose = jnp.where(wanted.astype(jnp.float32) == place, 1.0, 0.0).astype(jnp.bfloat16)
    rows = pl.ds(base, width)
    slot_mult = dot_nt(jnp.broadcast_to(mult.astype(jnp.bfloat16), (16, width)), choose)[0:1, :]
    far_keys_ref[...] = dot(choose, keys_ref[rows, :]).astype(jnp.bfloat16)
    distinct = jnp.sum(jnp.where(mult > 0.0, 1.0, 0.0), axis=1, keepdims=True)
    pieces = [slot_mult, coarse_mult, jnp.broadcast_to(distinct, (1, META_LANES - COUNT_LANE))]
    starts = [0, COARSE_LANE, COUNT_LANE, META_LANES]
    padded = [
        jnp.concatenate([x, jnp.zeros((1, end - start - x.shape[1]), jnp.float32)], axis=1)
        if end - start > x.shape[1]
        else x
        for x, start, end in zip(pieces, starts, starts[1:])
    ]
    meta = jnp.concatenate(padded, axis=1)
    first = lax.broadcasted_iota(jnp.int32, (16, META_LANES), 0) == 0
    old = far_keys_ref[0:16, 0:META_LANES].astype(jnp.float32)
    far_keys_ref[0:16, 0:META_LANES] = jnp.where(first, meta, old).astype(jnp.bfloat16)
    start = 0
    for ref in far_values_refs:
        cols = slice(start, start + ref.shape[1])
        ref[...] = dot(choose, values_ref[rows, cols]).astype(jnp.bfloat16)
        start = cols.stop


def head(h):
    return slice(h * HD, (h + 1) * HD)


def blank_rows(count):
    return [jnp.zeros((count, HD), jnp.bfloat16)] if count else []


def across_tiles(slab, columns):
    return jnp.concatenate([slab] * (columns // HD), axis=1)


def with_ones(values):
    return jnp.concatenate([values, jnp.ones_like(values)], axis=1)


def near_kernel(
    exact, half, first, index_ref, counts_ref, queries_ref, keys_ref, values_ref, near_ref, sums_ref, *high_ref
):
    rows, count = keys_ref.shape[0], index_ref.shape[1]
    band = lax.axis_index("band")
    odd = lax.rem(band, 2)
    meta = near_ref[near_ref.shape[0] - 16 :, 0:half].astype(jnp.float32)
    mult = multiplicity(meta[0:1, :], counts_ref[odd, band + 1 - 2 * odd])
    row = lax.broadcasted_iota(jnp.int32, (count, half), 1).astype(jnp.float32)
    among = jnp.where(column(meta[1:2, 0:count]) == row, 1.0, 0.0)
    bias = log_mult(mult + jnp.sum(among, axis=0, keepdims=True))
    own = jnp.where(lax.broadcasted_iota(jnp.int32, (rows, count), 0) == index_ref[...], 1.0, 0.0)
    own = 1.0 + jnp.sum(own, axis=1, keepdims=True)
    own = jnp.broadcast_to(own, (rows, HD)).astype(jnp.bfloat16)
    for h in range(sums_ref.shape[0]):
        cols = head(first + h)
        queries = queries_ref[:, cols]
        scores = [
            dot_nt(queries, keys_ref[:, cols]) * SCALE,
            dot_nt(queries, near_ref[0:half, cols]) * SCALE + bias,
        ]
        if exact:
            high = jnp.maximum(*[jnp.max(x, axis=1, keepdims=True) for x in scores])
            scores = [x - high for x in scores]
            high_ref[0][h] = jnp.broadcast_to(high, high_ref[0].shape[1:])
        weights = jnp.concatenate([jnp.exp2(x).astype(jnp.bfloat16) for x in scores], axis=1)
        values = jnp.concatenate([values_ref[:, cols] * own, own], axis=1)
        values = jnp.concatenate([values, with_ones(near_ref[half : 2 * half, cols])], axis=0)
        sums_ref[h] = dot(weights, values)


def far_kernel(exact, groups, half, count, queries_ref, sent_keys_ref, far_keys_ref, near_ref, *refs):
    sums_refs, (accum_ref, weights_ref, state_ref) = refs[:groups], refs[-3:]
    high_ref = refs[groups] if exact else None
    coarse_refs = refs[groups + exact : -3]
    rows = queries_ref.shape[0]
    slots = far_keys_ref.shape[0]
    padded = weights_ref.shape[2]
    bands = lax.axis_size("band")
    band = lax.axis_index("band")
    edge = (band == 0) | (band == bands - 1)

    def meta_of(ref):
        meta = ref[0:16, 0:META_LANES].astype(jnp.float32)
        first = lax.broadcasted_iota(jnp.int32, meta.shape, 0) == 0
        return jnp.sum(jnp.where(first, meta, 0.0), axis=0, keepdims=True)

    mult = jnp.where(edge, 0.0, meta_of(far_keys_ref))
    most = jnp.max(jnp.maximum(mult, meta_of(sent_keys_ref))[:, COUNT_LANE:])
    overflow = (most > slots - 1.0) & jnp.logical_not(edge)
    few = count // 2
    near = 2 * half + (1 - lax.rem(band, 2)) * few
    near_keys = pl.ds(pl.multiple_of(near, few), few)
    near_values = pl.ds(pl.multiple_of(near + count, few), few)
    coarse = few + len(coarse_refs) * count
    pad = padded - coarse - slots
    bias = [
        jnp.zeros((1, few), jnp.float32),
        jnp.log2(1.0 + mult[:, COARSE_LANE : COARSE_LANE + count]),
        jnp.zeros((1, coarse - few - count), jnp.float32),
        log_mult(mult[:, 0:slots]),
    ]
    bias = jnp.concatenate(bias + ([jnp.full((1, pad), DEAD, jnp.float32)] if pad else []), axis=1)
    no_keys = blank_rows(pad)
    no_values = blank_rows(padded - coarse)
    sizes = jnp.zeros((rows, HD), jnp.float32)
    for h in range(H):
        summed = sums_refs[h * groups // H][h % (H // groups)]
        cols = head(h)
        keys = [near_ref[near_keys, cols]] + [ref[0:count, cols] for ref in coarse_refs]
        keys = jnp.concatenate(keys + [far_keys_ref[:, cols]] + no_keys, axis=0)
        values = [near_ref[near_values, cols]] + [ref[count : 2 * count, cols] for ref in coarse_refs]
        values = jnp.concatenate(values + no_values, axis=0)
        scores = dot_nt(queries_ref[:, cols], keys) * SCALE + bias
        if exact:
            old = high_ref[h]
            high = jnp.maximum(old, jnp.max(scores, axis=1, keepdims=True))
            summed = summed * across_tiles(jnp.exp2(old - high), 2 * HD)
            scores = scores - across_tiles(high, padded)
        weights = jnp.exp2(scores)
        summed = summed + dot(weights.astype(jnp.bfloat16), with_ones(values))
        total = summed[:, HD:]
        inverse = 1.0 / total
        sizes = sizes + (total + inverse)
        accum_ref[:, cols] = summed[:, :HD] * inverse
        weights_ref[h] = (weights * across_tiles(inverse, padded)).astype(jnp.bfloat16)
    safe = jnp.max(sizes) < 2.0**60
    state = jnp.where(overflow, 2.0, jnp.where(safe | exact, 0.0, 1.0))
    state_ref[...] = jnp.broadcast_to(state, state_ref.shape)


def far_share(coarse, h, weights_ref, part, far_values):
    slots, padded = far_values.shape[0], weights_ref.shape[2]
    values = jnp.concatenate(blank_rows(coarse) + [far_values] + blank_rows(padded - coarse - slots), axis=0)
    return dot(weights_ref[h, part, :], values)


def early_kernel(coarse, state_in, accum_ref, weights_ref, far_values_ref, attended_ref, state_ref):
    everything = pl.ds(0, accum_ref.shape[0])
    state_ref[0] = jnp.max(state_in[...]).astype(jnp.int32)
    for h in range(far_values_ref.shape[1] // HD):
        cols = head(h)
        share = far_share(coarse, h, weights_ref, everything, far_values_ref[:, cols])
        attended_ref[:, cols] = accum_ref[:, cols] + share


def project_kernel(coarse, done, accum_ref, weights_ref, far_values_ref, gain_ref, matrix_ref, *refs):
    attended_ref, (out_hbm, normed_ref, out_ref, sems) = refs[0] if done else None, refs[-4:]
    rows, width = accum_ref.shape
    part_rows = rows // 2
    copies = []

    def attended(part, h):
        if h < done:
            return attended_ref[part, head(h)]
        share = far_share(coarse, h, weights_ref, part, far_values_ref[:, head(h - done)])
        return accum_ref[part, head(h)] + share

    def centred(heads):
        center = jnp.sum(functools.reduce(jnp.add, heads), axis=1, keepdims=True) * (1.0 / width)
        heads = [x - center for x in heads]
        square = functools.reduce(jnp.add, [x * x for x in heads])
        spread = jnp.sum(square, axis=1, keepdims=True) * (1.0 / width)
        return heads, lax.rsqrt(spread + 1e-05)

    def norm(part, heads, inverse):
        for h, x in enumerate(heads):
            normed_ref[part, head(h)] = (x * inverse * gain_ref[:, head(h)]).astype(jnp.bfloat16)

    def project(part, start, stop):
        cols = slice(start * width // 6, stop * width // 6)
        out_ref[part, cols] = dot(normed_ref[part, :], matrix_ref[:, cols]).astype(jnp.bfloat16)

    def send(part, start, stop):
        block = (part, pl.ds(start * width // 6, (stop - start) * width // 6))
        copies.append(pltpu.make_async_copy(out_ref.at[block], out_hbm.at[block], sems.at[len(copies)]))
        copies[-1].start()

    one, two = pl.ds(0, part_rows), pl.ds(part_rows, part_rows)
    norm(one, *centred([attended(one, h) for h in range(H)]))
    heads = []
    for i in range(3):
        heads += [attended(two, h) for h in range(4 * i, 4 * i + 4)]
        project(one, i, i + 1)
    heads, inverse = centred(heads)
    project(one, 3, 4)
    norm(two, heads, inverse)
    project(one, 4, 6)
    send(one, 0, 6)
    for i in range(0, 6, 2):
        project(two, i, i + 2)
        send(two, i, i + 2)
    for copy in copies:
        copy.wait()


def spec(space=VMEM):
    return pl.BlockSpec(memory_space=space)


def call(kernel, ins, outs, scratch=(), limit=24, cost=None):
    flops, nbytes, exps = cost
    ins = [(pltpu.with_memory_space_constraint(x, s) if s is pltpu.HBM else x, s) for x, s in ins]
    return pl.pallas_call(
        kernel,
        in_specs=[spec(s) for _, s in ins],
        out_specs=tuple(spec(SPACE.get(keep, VMEM)) for _, _, keep in outs),
        out_shape=tuple(
            MEMORY[keep](shape, dtype) for shape, dtype, keep in outs
        ),
        scratch_shapes=list(scratch),
        compiler_params=pltpu.CompilerParams(vmem_limit_bytes=limit << 20),
        cost_estimate=pl.CostEstimate(flops=flops, bytes_accessed=nbytes, transcendentals=exps),
    )(*[x for x, _ in ins])


def on_device(queries, keys, values, out_gain, out_weight, adjacency, send_counts, coarse_index):
    rows, width = queries.shape
    bands = lax.axis_size("band")
    half = adjacency.shape[2]
    count = coarse_index.shape[0]
    slots = (half * 21 // 32 if bands == 4 else half * 11 // 16) // 8 * 8
    bf16, f32 = jnp.bfloat16, jnp.float32
    smem = pltpu.SMEM

    def swap(block, mask):
        return lax.ppermute(block, "band", [(i, i ^ mask) for i in range(bands)])

    def far(block):
        slides = lax.axis_size("slide")
        pairs = []
        for slide in range(slides):
            for band in range(bands):
                end = band in (0, bands - 1)
                to = (slide ^ 1, band) if end else (slide, band + 1 if band % 2 else band - 1)
                pairs.append((slide * bands + band, to[0] * bands + to[1]))
        return lax.ppermute(block, ("slide", "band"), pairs)

    def across(block):
        up = [(i, i + 1) for i in range(1, bands - 1, 2)]
        return lax.ppermute(block, "band", up + [(j, i) for i, j in up])

    early = width * EARLY // H
    index = coarse_index.reshape(1, count)
    others = (bands - 2) * count + count // 2
    after = lambda first, x: lax.optimization_barrier((first, x))[1]
    resident = ((rows, width), bf16, "vmem")
    coarse, near, keys, values = call(
        coarse_kernel,
        [(x, pltpu.HBM) for x in (index, adjacency, keys, values)],
        [((2 * count, width), bf16, "any"), ((2 * (half + count) + 16, width), bf16, "any"), resident, resident],
        scratch=[
            pltpu.VMEM((1, count), jnp.int32),
            pltpu.VMEM(adjacency.shape, jnp.int32),
            pltpu.SemaphoreType.DMA((6,)),
        ],
        cost=(4 * count * rows * width, 4 * rows * width, 0),
    )
    mirrored = swap(coarse, bands - 1)
    near = swap(near, 1)
    send_counts = send_counts.T

    def boundary(slots):
        return call(
            functools.partial(boundary_kernel, bands == 4),
            [(index, VMEM), (adjacency, VMEM), (send_counts, smem), (keys, VMEM), (values, VMEM)],
            [((slots, columns), bf16, "any") for columns in (width, early, width - early)],
            cost=(1, 1, 0),
        )

    def near_sums(exact, keys, first, heads):
        wide = ((heads, rows, 2 * HD), f32, "vmem")
        return call(
            functools.partial(near_kernel, exact, half, first),
            [(index, VMEM), (send_counts, smem)] + [(x, VMEM) for x in [queries, keys, values, near]],
            [wide, ((heads, rows, HD), f32, "vmem")] if exact else [wide],
            cost=((21 if first else 0) * rows * half * width, 2, 0),
        )

    def far_weights(exact, states, sent_keys, far_keys):
        slots = far_keys.shape[0]
        padded = -(-(others + slots) // HD) * HD
        return call(
            functools.partial(far_kernel, exact, len(states) - exact, half, count),
            [(x, VMEM) for x in [queries, sent_keys, far_keys, near] + list(states) + pieces[1:]],
            [((rows, width), f32, "vmem"), ((H, rows, padded), bf16, "vmem"), ((8, HD), f32, "vmem")],
            cost=(4 * rows * slots * width, 2 * rows * width, H * rows * slots),
        )

    def project(done, accum, weights, far_values, *attended):
        operands = (accum, weights, far_values, gain, out_weight, *attended)
        return call(
            functools.partial(project_kernel, others, done),
            [(x, VMEM) for x in operands],
            [((rows, width), bf16, "hbm")],
            scratch=[
                pltpu.VMEM((rows, width), bf16),
                pltpu.VMEM((rows, width), bf16),
                pltpu.SemaphoreType.DMA((4,)),
            ],
            cost=(2 * rows * width * (half + width), 2 * width * width, 0),
        )[0]

    sent_keys, *sent_values = boundary(slots)
    far_keys = far(sent_keys)
    far_values = [far(sent_values[0])]
    own_keys = after(sent_keys, keys)
    half_heads = H // 2
    (first,) = near_sums(False, own_keys, 0, half_heads)
    mirrored = after(first, mirrored)
    (second,) = near_sums(False, after(mirrored, own_keys), half_heads, H - half_heads)
    states = [first, second]
    far_values.append(far(after(second, sent_values[1])))
    pieces = [coarse, mirrored, swap(mirrored, 1)]
    near_piece = near[2 * half : 2 * (half + count)] if bands > 4 else None
    for mask in [1 << i for i in range(1, bands.bit_length() - 2)]:
        pieces = pieces + [swap(piece, mask) for piece in pieces + [near_piece]]
    accum, weights, state = far_weights(False, states, sent_keys, far_keys)
    gain = after(accum, out_gain.reshape(1, width))
    attended, state = call(
        functools.partial(early_kernel, others),
        [(x, VMEM) for x in [state, accum, weights, far_values[0]]],
        [((rows, early), f32, "vmem"), ((1,), jnp.int32, "scalar")],
        cost=(16 * rows * slots * width, 2 * rows * early, 0),
    )

    def fine():
        return project(early // HD, accum, weights, far_values[1], attended)

    def exact():
        accum, weights, _ = far_weights(True, near_sums(True, keys, 0, H), sent_keys, far_keys)
        return project(0, accum, weights, jnp.concatenate(far_values, axis=1))

    def all_rows():
        sent_keys, *sent_values = boundary(half + 16)
        far_keys, far_values = across(sent_keys), across(jnp.concatenate(sent_values, axis=1))
        accum, weights, _ = far_weights(True, near_sums(True, keys, 0, H), sent_keys, far_keys)
        return project(0, accum, weights, far_values)

    return lax.switch(state[0], [fine, exact, all_rows])


def solution(mesh):
    in_specs = (
        P(("slide", "band"), None),
        P(("slide", "band"), None),
        P(("slide", "band"), None),
        P(),
        P(),
        P(("slide", "band"), None, None),
        P("slide", None),
        P(("slide", "band")),
    )
    out_specs = P(("slide", "band"), None)
    return jax.shard_map(
        on_device, mesh=mesh, in_specs=in_specs, out_specs=out_specs, check_vma=False
    )
```
